128 devices in a mesh: dp: 32 (over x, z, core), rows: 4 (over y).
Axes of the slice: x: 4, y: 4, z: 4, core: 2. Of those that a mesh axis runs over, the one named last changes fastest.
Arguments:
- images: bfloat16 [192, 32, 128, 256], P('dp', 'rows'), may hold values from -120 to 120
- kernel: bfloat16 [3, 3, 256, 128], replicated, may hold values from -0.25 to 0.25
- colors: float32 [2, 64, 64], replicated, may hold values from -0.75 to 0.75
- offset: float32 [128], replicated, may hold values from -4 to 4
- upstream: bfloat16 [192, 32, 128, 128], P('dp', 'rows'), may hold values from -8 to 8
Outputs:
- colored: bfloat16 [192, 32, 128, 128], P('dp', 'rows')
- grad_images: bfloat16 [192, 32, 128, 256], P('dp', 'rows')
- grad_kernel: float32 [3, 3, 256, 128], replicated
- grad_colors: float32 [2, 64, 64], replicated
The draws below stay inside these ranges and needn't reach their ends.
All inputs are finite; a program needn't handle non-finite values.
Results may differ from the reference program's by a relative error of at most 0.0044.
The reference program's roundings to bfloat16 on the way (of `pre_grad`) count: a program that leaves them out, or rounds other values in their place, can miss the bound.
Values may be sent and summed in bfloat16 or wider, within the bound.
A program may use at most 128 MiB of HBM per device.

```python
import math
import jax
import jax.numpy as jnp
from jax import lax

CIN = 256
COUT = 128
GS = 64
WID = 128
NS_ITERS = 5
BATCH = 192
HEIGHT = 32
GROUPS = 2


def picture(key):
    first = jax.random.fold_in(key, 11)
    second = jax.random.fold_in(key, 12)
    third = jax.random.fold_in(key, 13)
    image_pos = jnp.arange(BATCH, dtype=jnp.float32) / max(BATCH - 1, 1)
    row_pos = jnp.arange(HEIGHT, dtype=jnp.float32) / max(HEIGHT - 1, 1)
    scaling = (10.0 ** image_pos)[:, None, None, None] * (3.0 ** row_pos)[None, :, None, None]
    signs = jnp.where(jax.random.bernoulli(third, 0.5, (CIN,)), 1.0, -1.0).astype(jnp.float32)
    base = jax.random.truncated_normal(first, -3.0, 3.0, (BATCH, HEIGHT, WID, CIN), jnp.float32)
    means = jax.random.uniform(second, (CIN,), jnp.float32, 0.5, 1.0) * signs
    return ((base + means) * scaling).astype(jnp.bfloat16)


def filters(key):
    inner = jax.random.fold_in(key, 23)
    base = jax.random.truncated_normal(inner, -4.0, 4.0, (3, 3, CIN, COUT), jnp.float32)
    return (base * (9.0 * CIN) ** (-0.5)).astype(jnp.bfloat16)


def draw_images(key, part):
    return picture(key)


def draw_kernel(key, part):
    return filters(key)


def draw_upstream(key, part):
    source = picture(key)
    weights = filters(key)
    forward = lax.conv_general_dilated(source, weights, (1, 1), ((1, 1), (1, 1)), dimension_numbers=('NHWC', 'HWIO', 'NHWC'), preferred_element_type=jnp.float32)
    noise_key = jax.random.fold_in(key, 37)
    level_key = jax.random.fold_in(key, 41)
    sign_key = jax.random.fold_in(key, 43)
    signs = jnp.where(jax.random.bernoulli(sign_key, 0.5, (COUT,)), 1.0, -1.0).astype(jnp.float32)
    noise = jax.random.truncated_normal(noise_key, -4.0, 4.0, (BATCH, HEIGHT, WID, COUT), jnp.float32)
    levels = jax.random.uniform(level_key, (COUT,), jnp.float32, 0.3, 1.0)
    total = 0.6 / 9.0 * forward + noise + levels * signs
    return jnp.clip(total, -8.0, 8.0).astype(jnp.bfloat16)


def gaussian(rng, dims, deviation, most, held_as=jnp.bfloat16):
    values = jax.random.normal(rng, dims, jnp.float32) * deviation
    return jnp.minimum(jnp.maximum(values, -most), most).astype(held_as)


def setup_inputs(seed: int = 0) -> dict:
    keys = jax.random.split(jax.random.key(seed), 6)
    images = draw_images(jax.random.fold_in(keys[5], 71), 0)
    kernel = draw_kernel(jax.random.fold_in(keys[5], 71), 0)
    colors = gaussian(keys[2], (GROUPS, GS, GS), GS ** -0.5, 0.75, jnp.float32)
    offset = gaussian(keys[3], (COUT,), 1.0, 4.0, jnp.float32)
    upstream = draw_upstream(jax.random.fold_in(keys[5], 71), 0)
    return {"images": images, "kernel": kernel, "colors": colors, "offset": offset, "upstream": upstream}


EPSILON = 1e-05
PRECISE = lax.Precision.HIGHEST

def batched(left, right):
    return jnp.einsum('gij,gjk->gik', left, right, precision=PRECISE)

def inv_root(sigma_mat):
    traces = jnp.trace(sigma_mat, axis1=1, axis2=2)
    normed = sigma_mat / traces[:, None, None]
    estimate = jnp.broadcast_to(jnp.eye(sigma_mat.shape[-1], dtype=sigma_mat.dtype), sigma_mat.shape)
    for repeat in range(NS_ITERS):
        cubed = batched(batched(estimate, estimate), estimate)
        estimate = 1.5 * estimate - 0.5 * batched(cubed, normed)
    return estimate / jnp.sqrt(traces)[:, None, None]

def filter_same(source, weights):
    return lax.conv_general_dilated(source, weights, (1, 1), ((1, 1), (1, 1)), dimension_numbers=('NHWC', 'HWIO', 'NHWC'), preferred_element_type=jnp.float32)

def reference(images, kernel, colors, offset, upstream):
    pre = filter_same(images, kernel)
    pixels_all = pre.shape[0] * pre.shape[1] * pre.shape[2]
    raw_cols = pre.reshape(pixels_all, GROUPS, GS)
    average = lax.optimization_barrier(jnp.sum(raw_cols, axis=0)) / pixels_all
    centred = raw_cols - average
    identity = jnp.eye(GS, dtype=centred.dtype)
    sigma_mat = jnp.einsum('pgi,pgj->gij', centred, centred, precision=PRECISE) / pixels_all + EPSILON * identity
    whitener, pullback = jax.vjp(inv_root, sigma_mat)
    whitened = jnp.einsum('gij,pgj->pgi', whitener, centred, precision=PRECISE)
    colored = jnp.einsum('gij,pgj->pgi', colors, whitened, precision=PRECISE) + offset.reshape(GROUPS, GS)
    colored = colored.astype(jnp.bfloat16).reshape(pre.shape)
    upward = upstream.reshape(pixels_all, GROUPS, GS).astype(jnp.float32)
    up_total = lax.optimization_barrier(jnp.sum(upward, axis=0))
    color_sum = jnp.einsum('pgi,pgj->gij', upward, whitened, precision=PRECISE)
    white_grad = jnp.einsum('gji,pgj->pgi', colors, upward, precision=PRECISE)
    whiten_grad = jnp.einsum('pgi,pgj->gij', white_grad, centred, precision=PRECISE)
    sigma_grad, = pullback(whiten_grad)
    symmetric = sigma_grad + jnp.transpose(sigma_grad, (0, 2, 1))
    mean_grad = jnp.einsum('gji,gj->gi', colors, up_total, precision=PRECISE) / pixels_all
    centred_grad = jnp.einsum('gji,pgj->pgi', whitener, white_grad, precision=PRECISE)
    centred_grad = centred_grad + jnp.einsum('gij,pgj->pgi', symmetric, centred, precision=PRECISE) / pixels_all
    pre_grad = centred_grad - jnp.einsum('gji,gj->gi', whitener, mean_grad, precision=PRECISE)
    pre_grad = pre_grad.astype(jnp.bfloat16).reshape(pre.shape)
    flipped = jnp.transpose(kernel[::-1, ::-1], (0, 1, 3, 2))
    grad_images = filter_same(pre_grad, flipped).astype(jnp.bfloat16)
    padded = jnp.pad(images, ((0, 0), (1, 1), (1, 1), (0, 0)))
    grad_flat = pre_grad.reshape(-1, COUT)
    height_n = images.shape[1]
    width_n = images.shape[2]
    outer = []
    for row_off in range(3):
        inner = []
        for col_off in range(3):
            window = padded[:, row_off:row_off + height_n, col_off:col_off + width_n, :].reshape(-1, CIN)
            inner.append(lax.dot_general(window, grad_flat, (((0,), (0,)), ((), ())), preferred_element_type=jnp.float32))
        outer.append(jnp.stack(inner))
    scaling = 1.0 / math.sqrt(pixels_all)
    grad_kernel = jnp.stack(outer) * scaling
    grad_colors = color_sum * scaling
    return (colored, grad_images, grad_kernel, grad_colors)
```

```python
import functools
import math

import jax
import jax.numpy as jnp
from jax import lax
from jax.experimental import pallas as pl
from jax.experimental.pallas import tpu as pltpu
from jax.sharding import PartitionSpec as P

NS_ITERS = 5
EPSILON = 1e-05
PRECISE = lax.Precision.HIGHEST
BF16 = jnp.bfloat16
F32 = jnp.float32
MESH = pl.DeviceIdType.MESH

IMGS, BAND, WID, CIN, COUT, GS = 6, 8, 128, 256, 128, 64
RING = 4
OCT = 8
PIX = IMGS * BAND * WID
ONE_ROW = COUT * 3


def exact(left, right, dims=((1,), (0,))):
    return lax.dot_general(
        left, right, (dims, ((), ())), precision=PRECISE, preferred_element_type=F32
    )


def fast(left, right):
    return jnp.dot(left, right, preferred_element_type=F32)


def from_left(block):
    place = lax.broadcasted_iota(jnp.int32, block.shape, 0) % WID
    return jnp.where(place == 0, 0.0, pltpu.roll(block, 1, 0))


def from_right(block):
    place = lax.broadcasted_iota(jnp.int32, block.shape, 0) % WID
    return jnp.where(place == WID - 1, 0.0, pltpu.roll(block, block.shape[0] - 1, 0))


def pack(full):
    lane = lax.broadcasted_iota(jnp.int32, (GS, full.shape[1]), 1) % COUT
    return jnp.where(lane < GS, full[:GS], full[GS:])


def merged(buf, count, pixels, spare, place):
    rows = buf[0, 0:8]
    mean = buf[0, 8:16]
    for slot in range(1, count):
        rows = rows + buf[slot, 0:8]
        mean = mean + buf[slot, 8:16]
    mean = mean * (1.0 / count)
    index = lax.broadcasted_iota(jnp.int32, mean.shape, 0)
    apart = jnp.zeros_like(mean)
    for slot in range(count):
        apart = jnp.where(index == slot, buf[slot, 8:16] - mean, apart)
    between = pack(exact(apart[:, :COUT], apart, ((0,), (0,)))) * float(pixels)
    for slot in range(OCT):
        spare[slot] = between[slot * 8 : slot * 8 + 8]
    return rows + spare[place], mean


def upper(top):
    lane = lax.broadcasted_iota(jnp.int32, top.shape, 1)
    return jnp.concatenate([top, jnp.where(lane < GS, 0.0, pltpu.roll(top, GS, 1))], axis=0)


def diag_pair(first, second):
    zero = jnp.zeros((GS, GS), F32)
    return jnp.concatenate(
        [
            jnp.concatenate([first, zero], axis=1),
            jnp.concatenate([zero, second], axis=1),
        ],
        axis=0,
    )


def whiten_terms(packed, colors, total_pix):
    row = lax.broadcasted_iota(jnp.int32, (GS, GS), 0)
    col = lax.broadcasted_iota(jnp.int32, (GS, GS), 1)
    eye = jnp.where(row == col, 1.0, 0.0).astype(F32)
    cross = packed[:, COUT:].T
    tops, fulls, traces, crosses = [], [], [], []
    for group in range(2):
        sigma = packed[:, group * GS : (group + 1) * GS] * (1.0 / total_pix) + EPSILON * eye
        trace = jnp.sum(jnp.sum(sigma * eye, axis=1, keepdims=True), axis=0, keepdims=True)
        along = cross[group * GS : (group + 1) * GS]
        grad = exact(colors[group].T, along)
        tops.append(jnp.concatenate([sigma / trace, grad], axis=1))
        fulls.append(upper(tops[-1]))
        traces.append(trace)
        crosses.append(along)
    wide_eye = jnp.concatenate([eye, jnp.zeros((GS, GS), F32)], axis=1)
    states = [1.5 * wide_eye - 0.5 * top for top in tops]
    for _ in range(NS_ITERS - 1):
        squares = [exact(state, upper(state)) for state in states]
        by_normed = [exact(state, full) for state, full in zip(states, fulls)]
        cubes = [exact(square, upper(term)) for square, term in zip(squares, by_normed)]
        states = [1.5 * state - 0.5 * cube for state, cube in zip(states, cubes)]
    found = []
    for group in range(2):
        trace = traces[group]
        root = lax.rsqrt(trace)
        estimate, slope = states[group][:, :GS], states[group][:, GS:]
        normed, grad = tops[group][:, :GS], tops[group][:, GS:]
        scalar = slope * normed + 0.5 * grad * estimate
        scalar = jnp.sum(jnp.sum(scalar, axis=1, keepdims=True), axis=0, keepdims=True)
        sigma_grad = (slope - eye * scalar) * (root / trace)
        both = (sigma_grad + sigma_grad.T) * (1.0 / total_pix)
        whitener = estimate * root
        colored_by = exact(colors[group], whitener)
        color_sum = exact(crosses[group], whitener, ((1,), (1,)))
        found.append((colored_by, both, color_sum))
    return found


def block_kernel(
    total_pix,
    images,
    kernel,
    colors,
    offset,
    upstream,
    colored,
    grad_images,
    kernel_sum,
    color_grad,
    img,
    x3,
    pre,
    wf,
    wb,
    imgt,
    pg3,
    pg_halo,
    col_buf,
    gi_buf,
    sums,
    moments,
    rhi,
    rlo,
    consts,
    stat_src,
    stat_a,
    stat_y,
    stat_z,
    stat_all,
    spare,
    gk,
    rx0,
    rx1,
    acc1,
    rx2,
    rx3,
    ag2,
    ag1,
    load_sem,
    weight_sem,
    store_sem,
    halo_send,
    halo_recv,
    oct_send,
    oct_recv,
    line_send,
    line_recv,
    back_send,
    back_recv,
    pg_send,
    pg_recv,
    gk_core_send,
    gk_core_recv,
    gk_send,
    gk_recv,
):
    dp = lax.axis_index("dp")
    y = lax.axis_index("rows")
    x = dp // (RING * 2)
    z = (dp // 2) % RING
    core = dp % 2
    octet = x * 2 + core

    def oct_device(index):
        return (((index // 2) * RING + z) * 2 + index % 2, y)

    def along(axis, index):
        if axis == "x":
            return ((index * RING + z) * 2 + core, y)
        if axis == "y":
            return (dp, index)
        return ((x * RING + index) * 2 + core, y)

    spot = {"x": x, "y": y, "z": z}

    loads = [
        pltpu.make_async_copy(images.at[b], img.at[b, pl.ds(1, BAND)], load_sem.at[b])
        for b in range(IMGS)
    ]
    up_load = pltpu.make_async_copy(
        upstream, x3.at[:, :, :, pl.ds(2 * COUT, COUT)], load_sem.at[IMGS]
    )
    weight_loads = [
        pltpu.make_async_copy(
            kernel.at[a, c],
            wf.at[pl.ds(a * CIN, CIN), pl.ds(c * COUT, COUT)],
            weight_sem.at[a * 3 + c],
        )
        for a in range(3)
        for c in range(3)
    ]
    for copy in weight_loads:
        copy.start()
    for copy in loads:
        copy.start()
    up_load.start()

    barrier = pltpu.get_barrier_semaphore()
    for k in range(1, OCT):
        pl.semaphore_signal(
            barrier, inc=1, device_id=oct_device((octet + k) % OCT), device_id_type=MESH
        )
    for axis in ("y", "z"):
        for k in range(1, RING):
            pl.semaphore_signal(
                barrier,
                inc=1,
                device_id=along(axis, (spot[axis] + k) % RING),
                device_id_type=MESH,
            )
    pl.semaphore_wait(barrier, OCT - 1 + 2 * (RING - 1))

    halo_up = pltpu.make_async_remote_copy(
        src_ref=images.at[:, 0],
        dst_ref=img.at[:, BAND + 1],
        send_sem=halo_send.at[0],
        recv_sem=halo_recv.at[0],
        device_id=along("y", (y + RING - 1) % RING),
        device_id_type=MESH,
    )
    halo_down = pltpu.make_async_remote_copy(
        src_ref=images.at[:, BAND - 1],
        dst_ref=img.at[:, 0],
        send_sem=halo_send.at[1],
        recv_sem=halo_recv.at[1],
        device_id=along("y", (y + 1) % RING),
        device_id_type=MESH,
    )

    @pl.when(y > 0)
    def _():
        halo_up.start()

    @pl.when(y < RING - 1)
    def _():
        halo_down.start()

    @pl.when(y == 0)
    def _():
        img[:, 0] = jnp.zeros((IMGS, WID, CIN), BF16)
        pg3[:, 0] = jnp.zeros((IMGS, WID, ONE_ROW), BF16)

    @pl.when(y == RING - 1)
    def _():
        img[:, BAND + 1] = jnp.zeros((IMGS, WID, CIN), BF16)
        pg3[:, BAND + 1] = jnp.zeros((IMGS, WID, ONE_ROW), BF16)

    for copy in weight_loads:
        copy.wait()
    for copy in loads:
        copy.wait()

    sums[...] = jnp.zeros_like(sums)

    def conv(lhs):
        out = fast(lhs, wf[...])
        return (
            from_left(out[:, :COUT])
            + out[:, COUT : 2 * COUT]
            + from_right(out[:, 2 * COUT :])
        )

    def count_in(block):
        part = block.reshape(-1, 8, COUT).sum(axis=0)
        sums[:, :COUT] = sums[:, :COUT] + part

    inner = BAND - 2

    @pl.loop(0, IMGS)
    def _(b):
        lhs = jnp.concatenate(
            [img[b, pl.ds(1 + a, inner)].reshape(inner * WID, CIN) for a in range(3)], axis=1
        )
        block = conv(lhs)
        count_in(block)
        pre[b, pl.ds(1, inner)] = block.reshape(inner, WID, COUT)

    for a in range(3):
        for c in range(3):
            tap = wf[a * CIN : (a + 1) * CIN, c * COUT : (c + 1) * COUT]
            wb[a * ONE_ROW + c * COUT : a * ONE_ROW + (c + 1) * COUT, :] = tap.T
    up_load.wait()

    @pl.loop(0, IMGS)
    def _(b):
        for h in range(BAND):
            imgt[b, :, h * WID : (h + 1) * WID] = img[b, h + 1].T
        ups = x3[b, :, :, 2 * COUT :].reshape(-1, 8, COUT).astype(F32).sum(axis=0)
        sums[:, COUT:] = sums[:, COUT:] + ups

    @pl.when(y < RING - 1)
    def _():
        halo_up.wait_recv()

    @pl.when(y > 0)
    def _():
        halo_down.wait_recv()

    @pl.loop(0, IMGS)
    def _(b):
        lhs = jnp.concatenate(
            [
                jnp.concatenate([img[b, a], img[b, BAND - 1 + a]], axis=0)
                for a in range(3)
            ],
            axis=1,
        )
        block = conv(lhs)
        count_in(block)
        pre[b, 0] = block[:WID]
        pre[b, BAND - 1] = block[WID:]

    own = jnp.sum(sums[...], axis=0, keepdims=True) * (1.0 / PIX)
    own_mean = own[:, :COUT]
    moments[...] = jnp.zeros_like(moments)

    @pl.loop(0, IMGS)
    def _(b):
        apart = pre[b].reshape(BAND * WID, COUT) - own_mean
        high = apart.astype(BF16)
        low = (apart - high.astype(F32)).astype(BF16)
        x3[b, :, :, :COUT] = low.reshape(BAND, WID, COUT)
        x3[b, :, :, COUT : 2 * COUT] = high.reshape(BAND, WID, COUT)
        ups = x3[b, :, :, 2 * COUT :].reshape(BAND * WID, COUT)
        moments[...] = moments[...] + fast(high.T, jnp.concatenate([high, ups], axis=1))

    packed = pack(moments[...])
    wide_own = jnp.broadcast_to(own, (8, 2 * COUT))
    for slot in range(OCT):
        stat_src[slot, 0:8] = packed[slot * 8 : slot * 8 + 8]
        stat_src[slot, 8:16] = wide_own

    copies = []
    for k in range(1, OCT):
        target = (octet + k) % OCT
        copies.append(
            pltpu.make_async_remote_copy(
                src_ref=stat_src.at[target],
                dst_ref=stat_a.at[octet],
                send_sem=oct_send.at[k - 1],
                recv_sem=oct_recv.at[k - 1],
                device_id=oct_device(target),
                device_id_type=MESH,
            )
        )
    for copy in copies:
        copy.start()
    stat_a[octet] = stat_src[octet]
    for copy in copies:
        copy.wait()
    rows, mean = merged(stat_a, OCT, PIX, spare, octet)
    pixels = PIX * OCT
    for number, (axis, buf) in enumerate((("y", stat_y), ("z", stat_z))):
        me = spot[axis]
        buf[me, 0:8] = rows
        buf[me, 8:16] = mean
        copies = [
            pltpu.make_async_remote_copy(
                src_ref=buf.at[me],
                dst_ref=buf.at[me],
                send_sem=line_send.at[number, k - 1],
                recv_sem=line_recv.at[number, k - 1],
                device_id=along(axis, (me + k) % RING),
                device_id_type=MESH,
            )
            for k in range(1, RING)
        ]
        for copy in copies:
            copy.start()
        for copy in copies:
            copy.wait()
        rows, mean = merged(buf, RING, pixels, spare, octet)
        pixels = pixels * RING
    stat_all[octet, 0:8] = rows
    stat_all[octet, 8:16] = mean
    copies = [
        pltpu.make_async_remote_copy(
            src_ref=stat_all.at[octet],
            dst_ref=stat_all.at[octet],
            send_sem=back_send.at[k - 1],
            recv_sem=back_recv.at[k - 1],
            device_id=oct_device((octet + k) % OCT),
            device_id_type=MESH,
        )
        for k in range(1, OCT)
    ]
    for copy in copies:
        copy.start()
    for copy in copies:
        copy.wait()
    packed = jnp.concatenate([stat_all[slot, 0:8] for slot in range(OCT)], axis=0)
    all_mean = stat_all[0, 8:16]

    (t0, b0, s0), (t1, b1, s1) = whiten_terms(packed, colors, total_pix)
    color_grad[0] = s0 * (1.0 / math.sqrt(total_pix))
    color_grad[1] = s1 * (1.0 / math.sqrt(total_pix))
    by_x = jnp.concatenate([diag_pair(t0.T, t1.T), diag_pair(b0, b1)], axis=1)
    by_up = jnp.concatenate([jnp.zeros((COUT, COUT), F32), diag_pair(t0, t1)], axis=1)
    x_high, up_high = by_x.astype(BF16), by_up.astype(BF16)
    rhi[0:COUT] = x_high
    rhi[COUT : 2 * COUT] = x_high
    rhi[2 * COUT :] = up_high
    rlo[0:COUT] = (by_x - x_high.astype(F32)).astype(BF16)
    rlo[COUT:] = (by_up - up_high.astype(F32)).astype(BF16)
    shift = wide_own[:, :COUT] - all_mean[:, :COUT]
    level = exact(shift, by_x) - exact(all_mean[:, COUT:], by_up)
    consts[:, :COUT] = level[:, :COUT] + offset[...]
    consts[:, COUT:] = level[:, COUT:]

    def spread(block):
        return jnp.concatenate(
            [from_right(block).astype(BF16), block.astype(BF16), from_left(block).astype(BF16)],
            axis=1,
        )

    def finish(lhs):
        out = fast(lhs, rhi[...]) + fast(lhs[:, COUT:], rlo[...]) + consts[0:1, :]
        return out[:, :COUT].astype(BF16), spread(out[:, COUT:])

    @pl.loop(0, IMGS)
    def _(b):
        lhs = jnp.concatenate([x3[b, 0], x3[b, BAND - 1]], axis=0)
        shown, grads = finish(lhs)
        col_buf[b, 0] = shown[:WID]
        col_buf[b, BAND - 1] = shown[WID:]
        pg3[b, 1] = grads[:WID]
        pg3[b, BAND] = grads[WID:]

    pg_up = pltpu.make_async_remote_copy(
        src_ref=pg3.at[:, 1, :, pl.ds(COUT, COUT)],
        dst_ref=pg_halo.at[1],
        send_sem=pg_send.at[0],
        recv_sem=pg_recv.at[0],
        device_id=along("y", (y + RING - 1) % RING),
        device_id_type=MESH,
    )
    pg_down = pltpu.make_async_remote_copy(
        src_ref=pg3.at[:, BAND, :, pl.ds(COUT, COUT)],
        dst_ref=pg_halo.at[0],
        send_sem=pg_send.at[1],
        recv_sem=pg_recv.at[1],
        device_id=along("y", (y + 1) % RING),
        device_id_type=MESH,
    )

    @pl.when(y > 0)
    def _():
        pg_up.start()

    @pl.when(y < RING - 1)
    def _():
        pg_down.start()

    @pl.loop(0, IMGS)
    def _(b):
        shown, grads = finish(x3[b, pl.ds(1, inner)].reshape(inner * WID, 3 * COUT))
        col_buf[b, pl.ds(1, inner)] = shown.reshape(inner, WID, COUT)
        pg3[b, pl.ds(2, inner)] = grads.reshape(inner, WID, ONE_ROW)

    col_store = pltpu.make_async_copy(col_buf, colored, store_sem.at[IMGS])
    col_store.start()

    orders = (("x", "y", "z"), ("y", "z", "x"), ("z", "x", "y"))

    def weight_part(a):
        gk[a] = jnp.zeros((CIN, ONE_ROW), F32)

        @pl.loop(0, IMGS)
        def _(b):
            rhs = pg3[b, pl.ds(2 - a, BAND)].reshape(BAND * WID, ONE_ROW)
            gk[a] = gk[a] + fast(imgt[b], rhs)

    core_rows = CIN // 2
    ring_rows = core_rows // RING
    last_rows = ring_rows // RING
    other_core = (dp + 1 - 2 * core, y)

    def rows_at(start, size):
        return pl.ds(pl.multiple_of(start, size), size)

    def ring_copies(part, stage, src, dst):
        axis = orders[part][(0, 1, 2, 1, 0)[stage]]
        me = spot[axis]
        return [
            pltpu.make_async_remote_copy(
                src_ref=src((me + k) % RING),
                dst_ref=dst(k),
                send_sem=gk_send.at[part, stage, k - 1],
                recv_sem=gk_recv.at[part, stage, k - 1],
                device_id=along(axis, (me + k) % RING),
                device_id_type=MESH,
            )
            for k in range(1, RING)
        ]

    flying = {}

    def start(part, copies):
        for copy in copies:
            copy.start()
        flying[part] = copies

    def settle(part):
        for copy in flying[part]:
            copy.wait()

    def step(part, stage):
        first, second, third = (spot[axis] for axis in orders[part])
        mine = core * core_rows
        if stage > 0:
            settle(part)
        if stage == 0:
            start(
                part,
                [
                    pltpu.make_async_remote_copy(
                        src_ref=gk.at[part, rows_at((1 - core) * core_rows, core_rows)],
                        dst_ref=rx0.at[part],
                        send_sem=gk_core_send.at[part, 0],
                        recv_sem=gk_core_recv.at[part, 0],
                        device_id=other_core,
                        device_id_type=MESH,
                    )
                ],
            )
        elif stage == 1:
            here = rows_at(mine, core_rows)
            gk[part, here] = gk[part, here] + rx0[part]
            start(
                part,
                ring_copies(
                    part,
                    0,
                    lambda piece: gk.at[part, rows_at(mine + piece * ring_rows, ring_rows)],
                    lambda k: rx1.at[part, k - 1],
                ),
            )
        elif stage == 2:
            held = gk[part, rows_at(mine + first * ring_rows, ring_rows)]
            acc1[part] = held + rx1[part, 0] + rx1[part, 1] + rx1[part, 2]
            start(
                part,
                ring_copies(
                    part,
                    1,
                    lambda piece: acc1.at[part, rows_at(piece * last_rows, last_rows)],
                    lambda k: rx2.at[part, k - 1],
                ),
            )
        elif stage == 3:
            held = acc1[part, rows_at(second * last_rows, last_rows)]
            rx3[part, third] = held + rx2[part, 0] + rx2[part, 1] + rx2[part, 2]
            start(
                part,
                ring_copies(
                    part, 2, lambda piece: rx3.at[part, third], lambda k: rx3.at[part, third]
                ),
            )
        elif stage == 4:
            here = rows_at(second * last_rows, last_rows)
            ag2[part, here] = (rx3[part, 0] + rx3[part, 1]) + (rx3[part, 2] + rx3[part, 3])
            start(
                part,
                ring_copies(
                    part, 3, lambda piece: ag2.at[part, here], lambda k: ag2.at[part, here]
                ),
            )
        elif stage == 5:
            here = rows_at(mine + first * ring_rows, ring_rows)
            ag1[part, here] = ag2[part].astype(BF16)
            start(
                part,
                ring_copies(
                    part, 4, lambda piece: ag1.at[part, here], lambda k: ag1.at[part, here]
                ),
            )
        elif stage == 6:
            here = rows_at(mine, core_rows)
            start(
                part,
                [
                    pltpu.make_async_remote_copy(
                        src_ref=ag1.at[part, here],
                        dst_ref=ag1.at[part, here],
                        send_sem=gk_core_send.at[part, 1],
                        recv_sem=gk_core_recv.at[part, 1],
                        device_id=other_core,
                        device_id_type=MESH,
                    )
                ],
            )

    gi_stores = [
        pltpu.make_async_copy(gi_buf.at[b], grad_images.at[b], store_sem.at[b])
        for b in range(IMGS)
    ]

    def image_grad(b):
        half = BAND // 2

        @pl.loop(0, 2)
        def _(part):
            lhs = jnp.concatenate(
                [
                    pg3[b, pl.ds(part * half + 2 - a, half)].reshape(half * WID, ONE_ROW)
                    for a in range(3)
                ],
                axis=1,
            )
            out = fast(lhs, wb[...]).astype(BF16)
            gi_buf[b, pl.ds(part * half, half)] = out.reshape(half, WID, CIN)

        gi_stores[b].start()

    weight_part(1)
    step(1, 0)

    @pl.when(y < RING - 1)
    def _():
        pg_up.wait_recv()

        @pl.loop(0, IMGS)
        def _(b):
            pg3[b, BAND + 1] = spread(pg_halo[1, b].astype(F32))

    @pl.when(y > 0)
    def _():
        pg_down.wait_recv()

        @pl.loop(0, IMGS)
        def _(b):
            pg3[b, 0] = spread(pg_halo[0, b].astype(F32))

    weight_part(0)
    step(0, 0)
    step(1, 1)
    weight_part(2)
    step(2, 0)
    step(0, 1)
    step(1, 2)
    image_grad(0)
    step(2, 1)
    step(0, 2)
    step(1, 3)
    image_grad(1)
    step(2, 2)
    step(0, 3)
    step(1, 4)
    image_grad(2)
    step(2, 3)
    step(0, 4)
    step(1, 5)
    image_grad(3)
    step(2, 4)
    step(0, 5)
    step(1, 6)
    image_grad(4)
    step(2, 5)
    step(0, 6)
    image_grad(5)
    step(2, 6)
    for part in (1, 0, 2):
        settle(part)
    last = pltpu.make_async_copy(ag1, kernel_sum, store_sem.at[IMGS + 1])
    last.start()

    @pl.when(y > 0)
    def _():
        halo_up.wait_send()
        pg_up.wait_send()

    @pl.when(y < RING - 1)
    def _():
        halo_down.wait_send()
        pg_down.wait_send()

    col_store.wait()
    for copy in gi_stores:
        copy.wait()
    last.wait()


def body(images, kernel, colors, offset, upstream):
    total_pix = PIX * lax.axis_size("dp") * lax.axis_size("rows")
    anywhere = pl.BlockSpec(memory_space=pl.ANY)
    local = pl.BlockSpec(memory_space=pltpu.VMEM)
    dma = pltpu.SemaphoreType.DMA
    colored, grad_images, kernel_sum, color_grad = pl.pallas_call(
        functools.partial(block_kernel, total_pix),
        out_shape=(
            jax.ShapeDtypeStruct((IMGS, BAND, WID, COUT), BF16),
            jax.ShapeDtypeStruct((IMGS, BAND, WID, CIN), BF16),
            jax.ShapeDtypeStruct((3, CIN, ONE_ROW), BF16),
            jax.ShapeDtypeStruct((2, GS, GS), F32),
        ),
        in_specs=[anywhere, anywhere, local, local, anywhere],
        out_specs=(anywhere, anywhere, anywhere, local),
        scratch_shapes=[
            pltpu.VMEM((IMGS, BAND + 2, WID, CIN), BF16),
            pltpu.VMEM((IMGS, BAND, WID, 3 * COUT), BF16),
            pltpu.VMEM((IMGS, BAND, WID, COUT), F32),
            pltpu.VMEM((3 * CIN, ONE_ROW), BF16),
            pltpu.VMEM((3 * ONE_ROW, CIN), BF16),
            pltpu.VMEM((IMGS, CIN, BAND * WID), BF16),
            pltpu.VMEM((IMGS, BAND + 2, WID, ONE_ROW), BF16),
            pltpu.VMEM((2, IMGS, WID, COUT), BF16),
            pltpu.VMEM((IMGS, BAND, WID, COUT), BF16),
            pltpu.VMEM((IMGS, BAND, WID, CIN), BF16),
            pltpu.VMEM((8, 2 * COUT), F32),
            pltpu.VMEM((COUT, 2 * COUT), F32),
            pltpu.VMEM((3 * COUT, 2 * COUT), BF16),
            pltpu.VMEM((2 * COUT, 2 * COUT), BF16),
            pltpu.VMEM((8, 2 * COUT), F32),
            pltpu.VMEM((OCT, 16, 2 * COUT), F32),
            pltpu.VMEM((OCT, 16, 2 * COUT), F32),
            pltpu.VMEM((RING, 16, 2 * COUT), F32),
            pltpu.VMEM((RING, 16, 2 * COUT), F32),
            pltpu.VMEM((OCT, 16, 2 * COUT), F32),
            pltpu.VMEM((OCT, 8, 2 * COUT), F32),
            pltpu.VMEM((3, CIN, ONE_ROW), F32),
            pltpu.VMEM((3, CIN // 2, ONE_ROW), F32),
            pltpu.VMEM((3, RING - 1, CIN // 8, ONE_ROW), F32),
            pltpu.VMEM((3, CIN // 8, ONE_ROW), F32),
            pltpu.VMEM((3, RING - 1, CIN // 32, ONE_ROW), F32),
            pltpu.VMEM((3, RING, CIN // 32, ONE_ROW), F32),
            pltpu.VMEM((3, CIN // 8, ONE_ROW), F32),
            pltpu.VMEM((3, CIN, ONE_ROW), BF16),
            dma((IMGS + 1,)),
            dma((9,)),
            dma((IMGS + 2,)),
            dma((2,)),
            dma((2,)),
            dma((OCT - 1,)),
            dma((OCT - 1,)),
            dma((2, RING - 1)),
            dma((2, RING - 1)),
            dma((OCT - 1,)),
            dma((OCT - 1,)),
            dma((2,)),
            dma((2,)),
            dma((3, 2)),
            dma((3, 2)),
            dma((3, 5, RING - 1)),
            dma((3, 5, RING - 1)),
        ],
        compiler_params=pltpu.CompilerParams(
            collective_id=0, has_side_effects=True, vmem_limit_bytes=56 * 1024 * 1024
        ),
    )(images, kernel, colors, offset.reshape(1, COUT), upstream)
    scaling = 1.0 / math.sqrt(total_pix)
    taps = kernel_sum.reshape(3, CIN, 3, COUT).transpose(0, 2, 1, 3).astype(F32) * scaling
    return colored, grad_images, taps, color_grad


def solution(mesh):
    placed = (P("dp", "rows", None, None), P(), P(), P(), P("dp", "rows", None, None))
    return jax.shard_map(
        body,
        mesh=mesh,
        in_specs=placed,
        out_specs=(P("dp", "rows", None, None), P("dp", "rows", None, None), P(), P()),
        check_vma=False,
    )
```

```python
import functools
import math

import jax
import jax.numpy as jnp
from jax import lax
from jax.experimental import pallas as pl
from jax.experimental.pallas import tpu as pltpu
from jax.sharding import PartitionSpec as P

NS_ITERS = 5
EPSILON = 1e-05
PRECISE = lax.Precision.HIGHEST
BF16 = jnp.bfloat16
F32 = jnp.float32
MESH = pl.DeviceIdType.MESH

IMGS, BAND, WID, CIN, COUT, GS = 6, 8, 128, 256, 128, 64
RING = 4
OCT = 8
PLANE = 16
PIX = IMGS * BAND * WID
ONE_ROW = COUT * 3


def exact(left, right, dims=((1,), (0,))):
    return lax.dot_general(
        left, right, (dims, ((), ())), precision=PRECISE, preferred_element_type=F32
    )


def fast(left, right):
    return jnp.dot(left, right, preferred_element_type=F32)


def from_left(block):
    place = lax.broadcasted_iota(jnp.int32, block.shape, 0) % WID
    return jnp.where(place == 0, 0.0, pltpu.roll(block, 1, 0))


def from_right(block):
    place = lax.broadcasted_iota(jnp.int32, block.shape, 0) % WID
    return jnp.where(place == WID - 1, 0.0, pltpu.roll(block, block.shape[0] - 1, 0))


def pack(full):
    lane = lax.broadcasted_iota(jnp.int32, (GS, full.shape[1]), 1) % COUT
    return jnp.where(lane < GS, full[:GS], full[GS:])


def upper(top):
    lane = lax.broadcasted_iota(jnp.int32, top.shape, 1)
    return jnp.concatenate([top, jnp.where(lane < GS, 0.0, pltpu.roll(top, GS, 1))], axis=0)


def diag_pair(first, second):
    zero = jnp.zeros((GS, GS), F32)
    return jnp.concatenate(
        [
            jnp.concatenate([first, zero], axis=1),
            jnp.concatenate([zero, second], axis=1),
        ],
        axis=0,
    )


def whiten_terms(packed, colors, total_pix):
    row = lax.broadcasted_iota(jnp.int32, (GS, GS), 0)
    col = lax.broadcasted_iota(jnp.int32, (GS, GS), 1)
    eye = jnp.where(row == col, 1.0, 0.0).astype(F32)
    cross = packed[:, COUT:].T
    tops, fulls, traces, crosses = [], [], [], []
    for group in range(2):
        sigma = packed[:, group * GS : (group + 1) * GS] * (1.0 / total_pix) + EPSILON * eye
        trace = jnp.sum(jnp.sum(sigma * eye, axis=1, keepdims=True), axis=0, keepdims=True)
        along = cross[group * GS : (group + 1) * GS]
        grad = exact(colors[group].T, along)
        tops.append(jnp.concatenate([sigma / trace, grad], axis=1))
        fulls.append(upper(tops[-1]))
        traces.append(trace)
        crosses.append(along)
    wide_eye = jnp.concatenate([eye, jnp.zeros((GS, GS), F32)], axis=1)
    states = [1.5 * wide_eye - 0.5 * top for top in tops]
    for _ in range(NS_ITERS - 1):
        squares = [exact(state, upper(state)) for state in states]
        by_normed = [exact(state, full) for state, full in zip(states, fulls)]
        cubes = [exact(square, upper(term)) for square, term in zip(squares, by_normed)]
        states = [1.5 * state - 0.5 * cube for state, cube in zip(states, cubes)]
    found = []
    for group in range(2):
        trace = traces[group]
        root = lax.rsqrt(trace)
        estimate, slope = states[group][:, :GS], states[group][:, GS:]
        normed, grad = tops[group][:, :GS], tops[group][:, GS:]
        scalar = slope * normed + 0.5 * grad * estimate
        scalar = jnp.sum(jnp.sum(scalar, axis=1, keepdims=True), axis=0, keepdims=True)
        sigma_grad = (slope - eye * scalar) * (root / trace)
        both = (sigma_grad + sigma_grad.T) * (1.0 / total_pix)
        whitener = estimate * root
        colored_by = exact(colors[group], whitener)
        color_sum = exact(crosses[group], whitener, ((1,), (1,)))
        found.append((colored_by, both, color_sum))
    return found


def block_kernel(
    total_pix,
    images,
    kernel,
    colors_in,
    offset_in,
    upstream,
    colored,
    grad_images,
    kernel_grad,
    color_grad,
    img,
    x3,
    wf,
    wb,
    colors,
    offset,
    imgt,
    pg3,
    pg_halo,
    base,
    sums,
    moments,
    rhi,
    rlo,
    consts,
    stat_src,
    stat_a,
    stat_p,
    stat_all,
    gk,
    rx_core,
    rx_plane,
    rx_line,
    full,
    load_sem,
    weight_sem,
    halo_send,
    halo_recv,
    oct_send,
    oct_recv,
    plane_send,
    plane_recv,
    back_send,
    back_recv,
    pg_send,
    pg_recv,
    gk_core_send,
    gk_core_recv,
    gk_line_send,
    gk_line_recv,
    gk_plane_send,
    gk_plane_recv,
):
    dp = lax.axis_index("dp")
    y = lax.axis_index("rows")
    x = dp // (RING * 2)
    z = (dp // 2) % RING
    core = dp % 2
    octet = x * 2 + core
    spot = y * RING + z
    inner = BAND - 2
    has_up = y > 0
    has_down = y < RING - 1

    def remote(src, dst, send, recv, device):
        return pltpu.make_async_remote_copy(
            src_ref=src,
            dst_ref=dst,
            send_sem=send,
            recv_sem=recv,
            device_id=device,
            device_id_type=MESH,
        )

    def oct_device(index):
        return (((index // 2) * RING + z) * 2 + index % 2, y)

    def plane_device(index):
        return ((x * RING + index % RING) * 2 + core, index // RING)

    up_device = (dp, (y + RING - 1) % RING)
    down_device = (dp, (y + 1) % RING)
    other_core = (dp + 1 - 2 * core, y)

    weight_loads = [
        pltpu.make_async_copy(
            kernel.at[a, c],
            wf.at[pl.ds(a * CIN, CIN), pl.ds(c * COUT, COUT)],
            weight_sem.at[a * 3 + c],
        )
        for a in range(3)
        for c in range(3)
    ] + [
        pltpu.make_async_copy(colors_in, colors, weight_sem.at[9]),
        pltpu.make_async_copy(offset_in, offset, weight_sem.at[10]),
    ]

    def load(b):
        return pltpu.make_async_copy(images.at[b], img.at[b, pl.ds(1, BAND)], load_sem.at[b])

    up_load = pltpu.make_async_copy(
        upstream, x3.at[:, :, :, pl.ds(2 * COUT, COUT)], load_sem.at[IMGS]
    )

    barrier = pltpu.get_barrier_semaphore()
    for k in range(1, PLANE):
        pl.semaphore_signal(
            barrier, inc=1, device_id=plane_device((spot + k) % PLANE), device_id_type=MESH
        )
    for k in range(1, OCT):
        pl.semaphore_signal(
            barrier, inc=1, device_id=oct_device((octet + k) % OCT), device_id_type=MESH
        )
    for copy in weight_loads:
        copy.start()
    for b in range(IMGS):
        load(b).start()
    up_load.start()

    @pl.when(y == 0)
    def _():
        img[:, 0] = jnp.zeros((IMGS, WID, CIN), BF16)
        pg3[:, 0] = jnp.zeros((IMGS, WID, ONE_ROW), BF16)

    @pl.when(y == RING - 1)
    def _():
        img[:, BAND + 1] = jnp.zeros((IMGS, WID, CIN), BF16)
        pg3[:, BAND + 1] = jnp.zeros((IMGS, WID, ONE_ROW), BF16)

    sums[...] = jnp.zeros_like(sums)
    moments[...] = jnp.zeros_like(moments)
    pl.semaphore_wait(barrier, OCT - 1 + PLANE - 1)

    def halo_up(b):
        return remote(
            images.at[b, 0],
            img.at[b, BAND + 1],
            halo_send.at[0, b],
            halo_recv.at[0, b],
            up_device,
        )

    def halo_down(b):
        return remote(
            images.at[b, BAND - 1],
            img.at[b, 0],
            halo_send.at[1, b],
            halo_recv.at[1, b],
            down_device,
        )

    for b in range(IMGS):

        @pl.when(has_up)
        def _():
            halo_up(b).start()

        @pl.when(has_down)
        def _():
            halo_down(b).start()

    for copy in weight_loads:
        copy.wait()
    up_load.wait()

    def conv(lhs):
        out = fast(lhs, wf[...])
        return (
            from_left(out[:, :COUT])
            + out[:, COUT : 2 * COUT]
            + from_right(out[:, 2 * COUT :])
        )

    def absorb(block, ups):
        apart = block - base[0:1, :]
        high = apart.astype(BF16)
        low = (apart - high.astype(F32)).astype(BF16)
        sums[:, :COUT] = sums[:, :COUT] + apart.reshape(-1, 8, COUT).sum(axis=0)
        sums[:, COUT:] = sums[:, COUT:] + ups.astype(F32).reshape(-1, 8, COUT).sum(axis=0)
        moments[...] = moments[...] + fast(high.T, jnp.concatenate([high, ups], axis=1))
        return jnp.concatenate([low, high], axis=1)

    def inner_conv(b):
        load(b).wait()
        return conv(
            jnp.concatenate(
                [img[b, pl.ds(1 + a, inner)].reshape(inner * WID, CIN) for a in range(3)],
                axis=1,
            )
        )

    def inner_absorb(b, block):
        ups = x3[b, pl.ds(1, inner), :, 2 * COUT :].reshape(inner * WID, COUT)
        both = absorb(block, ups)
        x3[b, pl.ds(1, inner), :, : 2 * COUT] = both.reshape(inner, WID, 2 * COUT)

    first = inner_conv(0)
    base[...] = jnp.broadcast_to(
        jnp.sum(first, axis=0, keepdims=True) * (1.0 / (inner * WID)), (8, COUT)
    )
    inner_absorb(0, first)

    @pl.loop(1, IMGS)
    def _(b):
        inner_absorb(b, inner_conv(b))

    for a in range(3):
        for c in range(3):
            tap = wf[a * CIN : (a + 1) * CIN, c * COUT : (c + 1) * COUT]
            wb[a * ONE_ROW + c * COUT : a * ONE_ROW + (c + 1) * COUT, :] = tap.T
    for b in range(IMGS):
        for h in range(BAND):
            start = (b * BAND + h) * WID
            imgt[:, start : start + WID] = img[b, h + 1].T

    @pl.loop(0, IMGS)
    def _(b):
        @pl.when(has_down)
        def _():
            halo_up(b).wait_recv()

        @pl.when(has_up)
        def _():
            halo_down(b).wait_recv()

        block = conv(
            jnp.concatenate(
                [
                    jnp.concatenate([img[b, a], img[b, BAND - 1 + a]], axis=0)
                    for a in range(3)
                ],
                axis=1,
            )
        )
        ups = jnp.concatenate(
            [x3[b, 0, :, 2 * COUT :], x3[b, BAND - 1, :, 2 * COUT :]], axis=0
        )
        both = absorb(block, ups)
        x3[b, 0, :, : 2 * COUT] = both[:WID]
        x3[b, BAND - 1, :, : 2 * COUT] = both[WID:]

    own = jnp.sum(sums[...], axis=0, keepdims=True) * (1.0 / PIX)
    drift = own[:, :COUT]
    column = jnp.broadcast_to(drift, (COUT, COUT)).T
    packed = pack(
        moments[...] - float(PIX) * jnp.concatenate([column, column], axis=1) * own
    )
    own_mean = jnp.concatenate([drift + base[0:1, :], own[:, COUT:]], axis=1)
    wide_own = jnp.broadcast_to(own_mean, (8, 2 * COUT))
    for slot in range(OCT):
        stat_src[slot, 0:8] = packed[slot * 8 : slot * 8 + 8]
        stat_src[slot, 8:16] = wide_own

    copies = []
    for k in range(1, OCT):
        target = (octet + k) % OCT
        copies.append(
            remote(
                stat_src.at[target],
                stat_a.at[octet],
                oct_send.at[k - 1],
                oct_recv.at[k - 1],
                oct_device(target),
            )
        )
    for copy in copies:
        copy.start()
    stat_a[octet] = stat_src[octet]
    for copy in copies:
        copy.wait()
    rows = stat_a[0, 0:8]
    means = stat_a[0, 8:16]
    index = lax.broadcasted_iota(jnp.int32, means.shape, 0)
    for slot in range(1, OCT):
        rows = rows + stat_a[slot, 0:8]
        means = jnp.where(index == slot, stat_a[slot, 8:16], means)
    stat_p[spot, 0:8] = rows
    stat_p[spot, 8:16] = means
    copies = [
        remote(
            stat_p.at[spot],
            stat_p.at[spot],
            plane_send.at[k - 1],
            plane_recv.at[k - 1],
            plane_device((spot + k) % PLANE),
        )
        for k in range(1, PLANE)
    ]
    for copy in copies:
        copy.start()
    for copy in copies:
        copy.wait()
    rows = stat_p[0, 0:8]
    for slot in range(1, PLANE):
        rows = rows + stat_p[slot, 0:8]
    stat_all[octet] = rows
    copies = [
        remote(
            stat_all.at[octet],
            stat_all.at[octet],
            back_send.at[k - 1],
            back_recv.at[k - 1],
            oct_device((octet + k) % OCT),
        )
        for k in range(1, OCT)
    ]
    for copy in copies:
        copy.start()
    means = jnp.concatenate([stat_p[slot, 8:16] for slot in range(PLANE)], axis=0)
    count = OCT * PLANE
    all_mean = jnp.broadcast_to(
        jnp.sum(means, axis=0, keepdims=True) * (1.0 / count), (8, 2 * COUT)
    )
    apart = means - all_mean[0:1, :]
    between = pack(exact(apart[:, :COUT].T, apart)) * float(PIX)
    for copy in copies:
        copy.wait()
    packed = (
        jnp.concatenate([stat_all[slot] for slot in range(OCT)], axis=0) + between
    )

    (t0, b0, s0), (t1, b1, s1) = whiten_terms(packed, colors, total_pix)
    by_x = jnp.concatenate([diag_pair(t0.T, t1.T), diag_pair(b0, b1)], axis=1)
    by_up = jnp.concatenate([jnp.zeros((COUT, COUT), F32), diag_pair(t0, t1)], axis=1)
    x_high, up_high = by_x.astype(BF16), by_up.astype(BF16)
    rhi[0:COUT] = x_high
    rhi[COUT : 2 * COUT] = x_high
    rhi[2 * COUT :] = up_high
    rlo[0:COUT] = (by_x - x_high.astype(F32)).astype(BF16)
    rlo[COUT:] = (by_up - up_high.astype(F32)).astype(BF16)
    shift = base[...] - all_mean[:, :COUT]
    level = exact(shift, by_x) - exact(all_mean[:, COUT:], by_up)
    consts[:, :COUT] = level[:, :COUT] + offset[...]
    consts[:, COUT:] = level[:, COUT:]

    def spread(block):
        return jnp.concatenate(
            [from_right(block).astype(BF16), block.astype(BF16), from_left(block).astype(BF16)],
            axis=1,
        )

    def finish(lhs):
        out = fast(lhs, rhi[...]) + fast(lhs[:, COUT:], rlo[...]) + consts[0:1, :]
        return out[:, :COUT].astype(BF16), spread(out[:, COUT:])

    def pg_up(b):
        return remote(
            pg3.at[b, 1, :, pl.ds(COUT, COUT)],
            pg_halo.at[1, b],
            pg_send.at[0, b],
            pg_recv.at[0, b],
            up_device,
        )

    def pg_down(b):
        return remote(
            pg3.at[b, BAND, :, pl.ds(COUT, COUT)],
            pg_halo.at[0, b],
            pg_send.at[1, b],
            pg_recv.at[1, b],
            down_device,
        )

    @pl.loop(0, IMGS)
    def _(b):
        shown, grads = finish(jnp.concatenate([x3[b, 0], x3[b, BAND - 1]], axis=0))
        colored[b, 0] = shown[:WID]
        colored[b, BAND - 1] = shown[WID:]
        pg3[b, 1] = grads[:WID]
        pg3[b, BAND] = grads[WID:]

        @pl.when(has_up)
        def _():
            pg_up(b).start()

        @pl.when(has_down)
        def _():
            pg_down(b).start()

    @pl.loop(0, IMGS)
    def _(b):
        shown, grads = finish(x3[b, pl.ds(1, inner)].reshape(inner * WID, 3 * COUT))
        colored[b, pl.ds(1, inner)] = shown.reshape(inner, WID, COUT)
        pg3[b, pl.ds(2, inner)] = grads.reshape(inner, WID, ONE_ROW)

    color_grad[0] = s0 * (1.0 / math.sqrt(total_pix))
    color_grad[1] = s1 * (1.0 / math.sqrt(total_pix))

    def rows_product(image_row, grad_row, rows):
        lhs = jnp.concatenate(
            [
                imgt[:, (b * BAND + image_row) * WID : (b * BAND + image_row + rows) * WID]
                for b in range(IMGS)
            ],
            axis=1,
        )
        rhs = jnp.concatenate(
            [
                pg3[b, grad_row : grad_row + rows].reshape(rows * WID, ONE_ROW)
                for b in range(IMGS)
            ],
            axis=0,
        )
        return fast(lhs, rhs)

    half = CIN // 2
    piece = half // PLANE

    def rows_at(start, size):
        return pl.ds(pl.multiple_of(start, size), size)

    mine = rows_at(core * half, half)
    theirs = rows_at((1 - core) * half, half)
    my_piece = rows_at(core * half + spot * piece, piece)
    flying = {}

    def start(part, copies):
        for copy in copies:
            copy.start()
        flying[part] = copies

    def settle(part):
        for copy in flying[part]:
            copy.wait()

    def plane_copies(part, stage, src, dst):
        return [
            remote(
                src((spot + k) % PLANE),
                dst(k),
                gk_plane_send.at[part, stage, k - 1],
                gk_plane_recv.at[part, stage, k - 1],
                plane_device((spot + k) % PLANE),
            )
            for k in range(1, PLANE)
        ]

    def step(part, stage):
        if stage > 0:
            settle(part)
        if stage == 0:
            start(
                part,
                [
                    remote(
                        gk.at[part, theirs],
                        rx_core.at[part],
                        gk_core_send.at[part, 0],
                        gk_core_recv.at[part, 0],
                        other_core,
                    )
                ],
            )
        elif stage == 1:
            gk[part, mine] = gk[part, mine] + rx_core[part]
            start(
                part,
                plane_copies(
                    part,
                    0,
                    lambda spot: gk.at[part, rows_at(core * half + spot * piece, piece)],
                    lambda k: rx_plane.at[part, k - 1],
                ),
            )
        elif stage == 2:
            held = gk[part, my_piece]
            for k in range(PLANE - 1):
                held = held + rx_plane[part, k]
            rx_line[part, x] = held
            start(
                part,
                [
                    remote(
                        rx_line.at[part, x],
                        rx_line.at[part, x],
                        gk_line_send.at[part, k - 1],
                        gk_line_recv.at[part, k - 1],
                        oct_device(((x + k) % RING) * 2 + core),
                    )
                    for k in range(1, RING)
                ],
            )
        elif stage == 3:
            full[part, my_piece] = (rx_line[part, 0] + rx_line[part, 1]) + (
                rx_line[part, 2] + rx_line[part, 3]
            )
            start(
                part,
                plane_copies(
                    part,
                    1,
                    lambda spot: full.at[part, my_piece],
                    lambda k: full.at[part, my_piece],
                ),
            )
        elif stage == 4:
            start(
                part,
                [
                    remote(
                        full.at[part, mine],
                        full.at[part, mine],
                        gk_core_send.at[part, 1],
                        gk_core_recv.at[part, 1],
                        other_core,
                    )
                ],
            )
        elif stage == 5:
            for c in range(3):
                kernel_grad[part, c] = full[part, :, c * COUT : (c + 1) * COUT] * (
                    1.0 / math.sqrt(total_pix)
                )

    def image_grad(b):
        lhs = jnp.concatenate(
            [pg3[b, pl.ds(2 - a, BAND)].reshape(BAND * WID, ONE_ROW) for a in range(3)],
            axis=1,
        )
        grad_images[b] = fast(lhs, wb[...]).astype(BF16).reshape(BAND, WID, CIN)

    gk[1] = rows_product(0, 1, BAND)
    step(1, 0)
    gk[0] = rows_product(0, 2, BAND - 1)

    @pl.loop(0, IMGS)
    def _(b):
        @pl.when(has_down)
        def _():
            pg_up(b).wait_recv()
            pg3[b, BAND + 1] = spread(pg_halo[1, b].astype(F32))

    gk[0] = gk[0] + rows_product(BAND - 1, BAND + 1, 1)
    step(0, 0)
    step(1, 1)
    gk[2] = rows_product(1, 1, BAND - 1)

    @pl.loop(0, IMGS)
    def _(b):
        @pl.when(has_up)
        def _():
            pg_down(b).wait_recv()
            pg3[b, 0] = spread(pg_halo[0, b].astype(F32))

    gk[2] = gk[2] + rows_product(0, 0, 1)
    step(2, 0)
    step(0, 1)
    image_grad(0)
    step(2, 1)
    image_grad(1)
    step(1, 2)
    image_grad(2)
    image_grad(3)
    step(0, 2)
    image_grad(4)
    step(1, 3)
    image_grad(5)
    step(2, 2)
    step(0, 3)
    step(2, 3)
    step(1, 4)
    step(0, 4)
    step(1, 5)
    step(2, 4)
    step(0, 5)
    step(2, 5)

    @pl.loop(0, IMGS)
    def _(b):
        @pl.when(has_up)
        def _():
            halo_up(b).wait_send()
            pg_up(b).wait_send()

        @pl.when(has_down)
        def _():
            halo_down(b).wait_send()
            pg_down(b).wait_send()


def place_kernel(*refs):
    count = (len(refs) - 1) // 2
    copies = [
        pltpu.make_async_copy(refs[i], refs[count + i], refs[-1].at[i]) for i in range(count)
    ]
    for copy in copies:
        copy.start()
    for copy in copies:
        copy.wait()


def body(images, kernel, colors, offset, upstream):
    total_pix = PIX * lax.axis_size("dp") * lax.axis_size("rows")
    anywhere = pl.BlockSpec(memory_space=pl.ANY)
    outside = pl.BlockSpec(memory_space=pltpu.HBM)
    local = pl.BlockSpec(memory_space=pltpu.VMEM)
    dma = pltpu.SemaphoreType.DMA
    shapes = (
        jax.ShapeDtypeStruct((IMGS, BAND, WID, COUT), BF16),
        jax.ShapeDtypeStruct((IMGS, BAND, WID, CIN), BF16),
        jax.ShapeDtypeStruct((3, 3, CIN, COUT), F32),
        jax.ShapeDtypeStruct((2, GS, GS), F32),
    )
    results = pl.pallas_call(
        functools.partial(block_kernel, total_pix),
        out_shape=shapes,
        in_specs=[outside] * 5,
        out_specs=(local, local, local, local),
        scratch_shapes=[
            pltpu.VMEM((IMGS, BAND + 2, WID, CIN), BF16),
            pltpu.VMEM((IMGS, BAND, WID, 3 * COUT), BF16),
            pltpu.VMEM((3 * CIN, ONE_ROW), BF16),
            pltpu.VMEM((3 * ONE_ROW, CIN), BF16),
            pltpu.VMEM((2, GS, GS), F32),
            pltpu.VMEM((1, COUT), F32),
            pltpu.VMEM((CIN, PIX), BF16),
            pltpu.VMEM((IMGS, BAND + 2, WID, ONE_ROW), BF16),
            pltpu.VMEM((2, IMGS, WID, COUT), BF16),
            pltpu.VMEM((8, COUT), F32),
            pltpu.VMEM((8, 2 * COUT), F32),
            pltpu.VMEM((COUT, 2 * COUT), F32),
            pltpu.VMEM((3 * COUT, 2 * COUT), BF16),
            pltpu.VMEM((2 * COUT, 2 * COUT), BF16),
            pltpu.VMEM((8, 2 * COUT), F32),
            pltpu.VMEM((OCT, 16, 2 * COUT), F32),
            pltpu.VMEM((OCT, 16, 2 * COUT), F32),
            pltpu.VMEM((PLANE, 16, 2 * COUT), F32),
            pltpu.VMEM((OCT, 8, 2 * COUT), F32),
            pltpu.VMEM((3, CIN, ONE_ROW), F32),
            pltpu.VMEM((3, CIN // 2, ONE_ROW), F32),
            pltpu.VMEM((3, PLANE - 1, CIN // 32, ONE_ROW), F32),
            pltpu.VMEM((3, RING, CIN // 32, ONE_ROW), F32),
            pltpu.VMEM((3, CIN, ONE_ROW), F32),
            dma((IMGS + 1,)),
            dma((11,)),
            dma((2, IMGS)),
            dma((2, IMGS)),
            dma((OCT - 1,)),
            dma((OCT - 1,)),
            dma((PLANE - 1,)),
            dma((PLANE - 1,)),
            dma((OCT - 1,)),
            dma((OCT - 1,)),
            dma((2, IMGS)),
            dma((2, IMGS)),
            dma((3, 2)),
            dma((3, 2)),
            dma((3, RING - 1)),
            dma((3, RING - 1)),
            dma((3, 2, PLANE - 1)),
            dma((3, 2, PLANE - 1)),
        ],
        compiler_params=pltpu.CompilerParams(
            collective_id=0, has_side_effects=True, vmem_limit_bytes=40 * 1024 * 1024
        ),
    )(
        *[
            pltpu.with_memory_space_constraint(given, pltpu.HBM)
            for given in (images, kernel, colors, offset.reshape(1, COUT), upstream)
        ]
    )
    return pl.pallas_call(
        place_kernel,
        out_shape=shapes,
        in_specs=[anywhere] * 4,
        out_specs=(anywhere,) * 4,
        scratch_shapes=[dma((4,))],
        compiler_params=pltpu.CompilerParams(vmem_limit_bytes=1024 * 1024),
    )(*results)


def solution(mesh):
    placed = (P("dp", "rows", None, None), P(), P(), P(), P("dp", "rows", None, None))
    return jax.shard_map(
        body,
        mesh=mesh,
        in_specs=placed,
        out_specs=(P("dp", "rows", None, None), P("dp", "rows", None, None), P(), P()),
        check_vma=False,
    )
```

```python
import functools
import math

import jax
import jax.numpy as jnp
from jax import lax
from jax.experimental import pallas as pl
from jax.experimental.pallas import tpu as pltpu
from jax.sharding import PartitionSpec as P

NS_ITERS = 5
EPSILON = 1e-05
PRECISE = lax.Precision.HIGHEST
BF16 = jnp.bfloat16
F32 = jnp.float32
MESH = pl.DeviceIdType.MESH

IMGS, BAND, WID, CIN, COUT, GS = 6, 8, 128, 256, 128, 64
RING = 4
OCT = 8
PLANE = 16
PIX = IMGS * BAND * WID
ONE_ROW = COUT * 3


def exact(left, right, dims=((1,), (0,))):
    return lax.dot_general(
        left, right, (dims, ((), ())), precision=PRECISE, preferred_element_type=F32
    )


def fast(left, right):
    return jnp.dot(left, right, preferred_element_type=F32)


def from_left(block):
    place = lax.broadcasted_iota(jnp.int32, block.shape, 0) % WID
    return jnp.where(place == 0, 0.0, pltpu.roll(block, 1, 0))


def from_right(block):
    place = lax.broadcasted_iota(jnp.int32, block.shape, 0) % WID
    return jnp.where(place == WID - 1, 0.0, pltpu.roll(block, block.shape[0] - 1, 0))


def pack(full):
    lane = lax.broadcasted_iota(jnp.int32, (GS, full.shape[1]), 1) % COUT
    return jnp.where(lane < GS, full[:GS], full[GS:])


def upper(top):
    lane = lax.broadcasted_iota(jnp.int32, top.shape, 1)
    return jnp.concatenate([top, jnp.where(lane < GS, 0.0, pltpu.roll(top, GS, 1))], axis=0)


def diag_pair(first, second):
    zero = jnp.zeros((GS, GS), F32)
    return jnp.concatenate(
        [
            jnp.concatenate([first, zero], axis=1),
            jnp.concatenate([zero, second], axis=1),
        ],
        axis=0,
    )


def whiten_terms(packed, colors, total_pix, between):
    row = lax.broadcasted_iota(jnp.int32, (GS, GS), 0)
    col = lax.broadcasted_iota(jnp.int32, (GS, GS), 1)
    eye = jnp.where(row == col, 1.0, 0.0).astype(F32)
    cross = packed[:, COUT:].T
    tops, fulls, traces, crosses = [], [], [], []
    for group in range(2):
        sigma = packed[:, group * GS : (group + 1) * GS] * (1.0 / total_pix) + EPSILON * eye
        trace = jnp.sum(jnp.sum(sigma * eye, axis=1, keepdims=True), axis=0, keepdims=True)
        along = cross[group * GS : (group + 1) * GS]
        grad = exact(colors[group].T, along)
        tops.append(jnp.concatenate([sigma / trace, grad], axis=1))
        fulls.append(upper(tops[-1]))
        traces.append(trace)
        crosses.append(along)
    wide_eye = jnp.concatenate([eye, jnp.zeros((GS, GS), F32)], axis=1)
    states = [1.5 * wide_eye - 0.5 * top for top in tops]
    for repeat in range(NS_ITERS - 1):
        if repeat == 2:
            between()
        squares = [exact(state, upper(state)) for state in states]
        by_normed = [exact(state, full) for state, full in zip(states, fulls)]
        cubes = [exact(square, upper(term)) for square, term in zip(squares, by_normed)]
        states = [1.5 * state - 0.5 * cube for state, cube in zip(states, cubes)]
    found = []
    for group in range(2):
        trace = traces[group]
        root = lax.rsqrt(trace)
        estimate, slope = states[group][:, :GS], states[group][:, GS:]
        normed, grad = tops[group][:, :GS], tops[group][:, GS:]
        scalar = slope * normed + 0.5 * grad * estimate
        scalar = jnp.sum(jnp.sum(scalar, axis=1, keepdims=True), axis=0, keepdims=True)
        sigma_grad = (slope - eye * scalar) * (root / trace)
        both = (sigma_grad + sigma_grad.T) * (1.0 / total_pix)
        whitener = estimate * root
        colored_by = exact(colors[group], whitener)
        color_sum = exact(crosses[group], whitener, ((1,), (1,)))
        found.append((colored_by, both, color_sum))
    return found


def block_kernel(
    total_pix,
    images,
    kernel,
    colors_in,
    offset_in,
    upstream,
    colored,
    grad_images,
    kernel_grad,
    color_grad,
    img,
    x3,
    wf,
    wb,
    colors,
    offset,
    imgt,
    window,
    window_col,
    pg3,
    pg_halo,
    base,
    sums,
    moments,
    rhi,
    rlo,
    mix,
    consts,
    stat_src,
    stat_a,
    stat_p,
    stat_all,
    spare,
    gk,
    rx_core,
    rx_first,
    held,
    rx_second,
    rx_third,
    full,
    load_sem,
    weight_sem,
    halo_send,
    halo_recv,
    oct_send,
    oct_recv,
    plane_send,
    plane_recv,
    back_send,
    back_recv,
    pg_send,
    pg_recv,
    gk_core_send,
    gk_core_recv,
    gk_line_send,
    gk_line_recv,
):
    dp = lax.axis_index("dp")
    y = lax.axis_index("rows")
    x = dp // (RING * 2)
    z = (dp // 2) % RING
    core = dp % 2
    octet = x * 2 + core
    spot = y * RING + z
    inner = BAND - 2
    has_up = y > 0
    has_down = y < RING - 1

    def remote(src, dst, send, recv, device):
        return pltpu.make_async_remote_copy(
            src_ref=src,
            dst_ref=dst,
            send_sem=send,
            recv_sem=recv,
            device_id=device,
            device_id_type=MESH,
        )

    def oct_device(index):
        return (((index // 2) * RING + z) * 2 + index % 2, y)

    def plane_device(index):
        return ((x * RING + index % RING) * 2 + core, index // RING)

    up_device = (dp, (y + RING - 1) % RING)
    down_device = (dp, (y + 1) % RING)
    other_core = (dp + 1 - 2 * core, y)

    weight_loads = [
        pltpu.make_async_copy(
            kernel.at[a, c],
            wf.at[pl.ds(a * CIN, CIN), pl.ds(c * COUT, COUT)],
            weight_sem.at[a * 3 + c],
        )
        for a in range(3)
        for c in range(3)
    ] + [
        pltpu.make_async_copy(colors_in, colors, weight_sem.at[9]),
        pltpu.make_async_copy(offset_in, offset, weight_sem.at[10]),
    ]

    def load(b):
        return pltpu.make_async_copy(images.at[b], img.at[b, pl.ds(1, BAND)], load_sem.at[b])

    up_load = pltpu.make_async_copy(
        upstream, x3.at[:, :, :, pl.ds(2 * COUT, COUT)], load_sem.at[IMGS]
    )

    barrier = pltpu.get_barrier_semaphore()
    for k in range(1, PLANE):
        pl.semaphore_signal(
            barrier, inc=1, device_id=plane_device((spot + k) % PLANE), device_id_type=MESH
        )
    for k in range(1, OCT):
        pl.semaphore_signal(
            barrier, inc=1, device_id=oct_device((octet + k) % OCT), device_id_type=MESH
        )
    for copy in weight_loads:
        copy.start()
    for b in range(IMGS):
        load(b).start()
    up_load.start()

    @pl.when(y == 0)
    def _():
        img[:, 0] = jnp.zeros((IMGS, WID, CIN), BF16)
        pg3[:, 0] = jnp.zeros((IMGS, WID, ONE_ROW), BF16)

    @pl.when(y == RING - 1)
    def _():
        img[:, BAND + 1] = jnp.zeros((IMGS, WID, CIN), BF16)
        pg3[:, BAND + 1] = jnp.zeros((IMGS, WID, ONE_ROW), BF16)

    sums[...] = jnp.zeros_like(sums)
    moments[...] = jnp.zeros_like(moments)
    pl.semaphore_wait(barrier, OCT - 1 + PLANE - 1)

    def halo_up(b):
        return remote(
            images.at[b, 0],
            img.at[b, BAND + 1],
            halo_send.at[0, b],
            halo_recv.at[0, b],
            up_device,
        )

    def halo_down(b):
        return remote(
            images.at[b, BAND - 1],
            img.at[b, 0],
            halo_send.at[1, b],
            halo_recv.at[1, b],
            down_device,
        )

    for b in range(IMGS):

        @pl.when(has_up)
        def _():
            halo_up(b).start()

        @pl.when(has_down)
        def _():
            halo_down(b).start()

    for copy in weight_loads:
        copy.wait()
    up_load.wait()

    def conv(lhs):
        out = fast(lhs, wf[...])
        return (
            from_left(out[:, :COUT])
            + out[:, COUT : 2 * COUT]
            + from_right(out[:, 2 * COUT :])
        )

    def absorb(block, ups):
        apart = block - base[0:1, :]
        high = apart.astype(BF16)
        low = (apart - high.astype(F32)).astype(BF16)
        sums[:, :COUT] = sums[:, :COUT] + apart.reshape(-1, 8, COUT).sum(axis=0)
        sums[:, COUT:] = sums[:, COUT:] + ups.astype(F32).reshape(-1, 8, COUT).sum(axis=0)
        moments[...] = moments[...] + fast(high.T, jnp.concatenate([high, ups], axis=1))
        return jnp.concatenate([low, high], axis=1)

    def inner_conv(b):
        load(b).wait()
        return conv(
            jnp.concatenate(
                [img[b, pl.ds(1 + a, inner)].reshape(inner * WID, CIN) for a in range(3)],
                axis=1,
            )
        )

    def inner_absorb(b, block):
        ups = x3[b, pl.ds(1, inner), :, 2 * COUT :].reshape(inner * WID, COUT)
        both = absorb(block, ups)
        x3[b, pl.ds(1, inner), :, : 2 * COUT] = both.reshape(inner, WID, 2 * COUT)

    first = inner_conv(0)
    base[...] = jnp.broadcast_to(
        jnp.sum(first, axis=0, keepdims=True) * (1.0 / (inner * WID)), (8, COUT)
    )
    inner_absorb(0, first)

    @pl.loop(1, IMGS)
    def _(b):
        inner_absorb(b, inner_conv(b))

    for a in range(3):
        for c in range(3):
            tap = wf[a * CIN : (a + 1) * CIN, c * COUT : (c + 1) * COUT]
            wb[a * ONE_ROW + c * COUT : a * ONE_ROW + (c + 1) * COUT, :] = tap.T
    window[...] = jnp.zeros_like(window)

    def turn(b, row):
        values = img[b, row].astype(F32)
        for c, moved in enumerate((from_left(values), values, from_right(values))):
            imgt[b, row, c * CIN : (c + 1) * CIN, :] = moved.astype(BF16).T
            window[row, c] = window[row, c] + moved.reshape(-1, 8, CIN).sum(axis=0)

    @pl.loop(0, IMGS)
    def _(b):
        for row in range(1, BAND + 1):
            turn(b, row)

    @pl.loop(0, IMGS)
    def _(b):
        @pl.when(has_down)
        def _():
            halo_up(b).wait_recv()

        @pl.when(has_up)
        def _():
            halo_down(b).wait_recv()

        block = conv(
            jnp.concatenate(
                [
                    jnp.concatenate([img[b, a], img[b, BAND - 1 + a]], axis=0)
                    for a in range(3)
                ],
                axis=1,
            )
        )
        ups = jnp.concatenate(
            [x3[b, 0, :, 2 * COUT :], x3[b, BAND - 1, :, 2 * COUT :]], axis=0
        )
        both = absorb(block, ups)
        x3[b, 0, :, : 2 * COUT] = both[:WID]
        x3[b, BAND - 1, :, : 2 * COUT] = both[WID:]
        turn(b, 0)
        turn(b, BAND + 1)

    orders = (("x", "y", "z"), ("y", "z", "x"), ("z", "x", "y"))
    where = {"x": x, "y": y, "z": z}
    half = 3 * CIN // 2
    quarter = half // RING
    piece = quarter // RING

    def rows_at(start, size):
        return pl.ds(pl.multiple_of(start, 8), size)

    def axis_device(axis, index):
        if axis == "x":
            return oct_device(index * 2 + core)
        return plane_device(index * RING + z if axis == "y" else y * RING + index)

    mine = rows_at(core * half, half)
    theirs = rows_at((1 - core) * half, half)
    flying = {}

    def start(part, copies):
        for copy in copies:
            copy.start()
        flying[part] = copies

    def settle(part):
        for copy in flying[part]:
            copy.wait()

    def line_copies(part, stage, src, dst):
        axis = orders[part][(0, 1, 2, 1, 0)[stage]]
        me = where[axis]
        return [
            remote(
                src((me + k) % RING),
                dst(k),
                gk_line_send.at[part, stage, k - 1],
                gk_line_recv.at[part, stage, k - 1],
                axis_device(axis, (me + k) % RING),
            )
            for k in range(1, RING)
        ]

    def step(part, stage):
        first, second, third = (where[axis] for axis in orders[part])
        my_quarter = rows_at(core * half + first * quarter, quarter)
        my_piece = rows_at(core * half + first * quarter + second * piece, piece)
        if stage > 0:
            settle(part)
        if stage == 0:
            start(
                part,
                [
                    remote(
                        gk.at[part, theirs],
                        rx_core.at[part],
                        gk_core_send.at[part, 0],
                        gk_core_recv.at[part, 0],
                        other_core,
                    )
                ],
            )
        elif stage == 1:
            gk[part, mine] = gk[part, mine] + rx_core[part]
            start(
                part,
                line_copies(
                    part,
                    0,
                    lambda index: gk.at[part, rows_at(core * half + index * quarter, quarter)],
                    lambda k: rx_first.at[part, k - 1],
                ),
            )
        elif stage == 2:
            held[part] = (
                (gk[part, my_quarter] + rx_first[part, 0])
                + (rx_first[part, 1] + rx_first[part, 2])
            )
            start(
                part,
                line_copies(
                    part,
                    1,
                    lambda index: held.at[part, rows_at(index * piece, piece)],
                    lambda k: rx_second.at[part, k - 1],
                ),
            )
        elif stage == 3:
            rx_third[part, third] = (
                (held[part, rows_at(second * piece, piece)] + rx_second[part, 0])
                + (rx_second[part, 1] + rx_second[part, 2])
            )
            start(
                part,
                line_copies(
                    part,
                    2,
                    lambda index: rx_third.at[part, third],
                    lambda k: rx_third.at[part, third],
                ),
            )
        elif stage == 4:
            total = (rx_third[part, 0] + rx_third[part, 1]) + (
                rx_third[part, 2] + rx_third[part, 3]
            )
            full[part, my_piece] = (
                exact(total, mix[0 : 2 * COUT])
                + window_col[part, my_piece] * mix[2 * COUT : 2 * COUT + 1]
            )
            start(
                part,
                line_copies(
                    part,
                    3,
                    lambda index: full.at[part, my_piece],
                    lambda k: full.at[part, my_piece],
                ),
            )
        elif stage == 5:
            start(
                part,
                line_copies(
                    part,
                    4,
                    lambda index: full.at[part, my_quarter],
                    lambda k: full.at[part, my_quarter],
                ),
            )
        elif stage == 6:
            start(
                part,
                [
                    remote(
                        full.at[part, mine],
                        full.at[part, mine],
                        gk_core_send.at[part, 1],
                        gk_core_recv.at[part, 1],
                        other_core,
                    )
                ],
            )
        elif stage == 7:
            for c in range(3):
                kernel_grad[part, c] = full[part, c * CIN : (c + 1) * CIN] * (
                    1.0 / math.sqrt(total_pix)
                )

    own = jnp.sum(sums[...], axis=0, keepdims=True) * (1.0 / PIX)
    drift = own[:, :COUT]
    column = jnp.broadcast_to(drift, (COUT, COUT)).T
    packed = pack(
        moments[...] - float(PIX) * jnp.concatenate([column, column], axis=1) * own
    )
    own_mean = jnp.concatenate([drift + base[0:1, :], own[:, COUT:]], axis=1)
    index = lax.broadcasted_iota(jnp.int32, (8, 2 * COUT), 0)
    taps = []
    for a in range(3):
        for c in range(3):
            total = window[a, c]
            for row in range(a + 1, a + BAND):
                total = total + window[row, c]
            taps.append(jnp.sum(total, axis=0, keepdims=True))
    taps = taps + [jnp.zeros_like(taps[0])] * (2 * OCT - len(taps))
    for slot in range(OCT):
        stat_src[slot, 0:8] = packed[slot * 8 : slot * 8 + 8]
        tail = jnp.where(index == 0, own_mean, 0.0)
        tail = jnp.where(index == 1, taps[2 * slot], tail)
        stat_src[slot, 8:16] = jnp.where(index == 2, taps[2 * slot + 1], tail)

    def columns_of(rows):
        place = lax.broadcasted_iota(jnp.int32, (2 * OCT, CIN), 0)
        stacked = jnp.zeros((2 * OCT, CIN), F32)
        for tap in range(9):
            stacked = jnp.where(place == tap, rows[tap], stacked)
        return stacked.T

    round_one = []
    for k in range(1, OCT):
        target = (octet + k) % OCT
        round_one.append(
            remote(
                stat_src.at[target],
                stat_a.at[octet],
                oct_send.at[k - 1],
                oct_recv.at[k - 1],
                oct_device(target),
            )
        )
    for copy in round_one:
        copy.start()
    stat_a[octet] = stat_src[octet]

    own_cols = columns_of(taps)

    def weight_part(a):
        lhs = jnp.concatenate([imgt[b, a + h] for b in range(IMGS) for h in range(BAND)], axis=1)
        gk[a] = fast(lhs, x3[:, :, :, COUT:].reshape(PIX, 2 * COUT))
        for c in range(3):
            column = own_cols[:, a * 3 + c : a * 3 + c + 1]
            rows = slice(c * CIN, (c + 1) * CIN)
            gk[a, rows, :COUT] = gk[a, rows, :COUT] + column * base[0:1, :]

    weight_part(1)
    step(1, 0)
    weight_part(0)
    step(0, 0)
    for copy in round_one:
        copy.wait()

    def spread_of(means, pixels):
        middle = jnp.sum(means, axis=0, keepdims=True) * (1.0 / means.shape[0])
        apart = means - middle
        return middle, pack(exact(apart[:, :COUT].T, apart)) * float(pixels)

    def tails_of(buf, count):
        place = lax.broadcasted_iota(jnp.int32, (count, 2 * COUT), 0)
        rows, tail = buf[0, 0:8], buf[0, 8:16]
        means = jnp.broadcast_to(buf[0, 8:9], (count, 2 * COUT))
        for slot in range(1, count):
            rows = rows + buf[slot, 0:8]
            tail = tail + buf[slot, 8:16]
            means = jnp.where(place == slot, buf[slot, 8:9], means)
        return rows, tail, means

    rows, tail, means = tails_of(stat_a, OCT)
    middle, between = spread_of(means, PIX)
    for slot in range(OCT):
        spare[slot] = between[slot * 8 : slot * 8 + 8]
    stat_p[spot, 0:8] = rows + spare[octet]
    stat_p[spot, 8:16] = jnp.where(index == 0, middle, tail)
    round_two = [
        remote(
            stat_p.at[spot],
            stat_p.at[spot],
            plane_send.at[k - 1],
            plane_recv.at[k - 1],
            plane_device((spot + k) % PLANE),
        )
        for k in range(1, PLANE)
    ]
    for copy in round_two:
        copy.start()
    step(1, 1)
    weight_part(2)
    step(2, 0)
    step(0, 1)
    step(2, 1)
    for copy in round_two:
        copy.wait()
    rows, tail, means = tails_of(stat_p, PLANE)
    stat_all[octet, 0:8] = rows
    stat_all[octet, 8:16] = tail
    round_three = [
        remote(
            stat_all.at[octet],
            stat_all.at[octet],
            back_send.at[k - 1],
            back_recv.at[k - 1],
            oct_device((octet + k) % OCT),
        )
        for k in range(1, OCT)
    ]
    for copy in round_three:
        copy.start()
    step(1, 2)
    middle, between = spread_of(means, PIX * OCT)
    all_mean = jnp.broadcast_to(middle, (8, 2 * COUT))
    step(0, 2)
    for copy in round_three:
        copy.wait()
    packed = jnp.concatenate([stat_all[slot, 0:8] for slot in range(OCT)], axis=0) + between
    all_cols = columns_of([stat_all[tap // 2, 9 + tap % 2 : 10 + tap % 2] for tap in range(9)])
    for a in range(3):
        for c in range(3):
            window_col[a, c * CIN : (c + 1) * CIN, :] = jnp.broadcast_to(
                all_cols[:, a * 3 + c : a * 3 + c + 1], (CIN, COUT)
            )

    step(2, 2)
    step(1, 3)

    (t0, b0, s0), (t1, b1, s1) = whiten_terms(
        packed, colors, total_pix, lambda: step(0, 3)
    )
    by_x = jnp.concatenate([diag_pair(t0.T, t1.T), diag_pair(b0, b1)], axis=1)
    by_up = jnp.concatenate([jnp.zeros((COUT, COUT), F32), diag_pair(t0, t1)], axis=1)
    x_high, up_high = by_x.astype(BF16), by_up.astype(BF16)
    rhi[0:COUT] = x_high
    rhi[COUT : 2 * COUT] = x_high
    rhi[2 * COUT :] = up_high
    rlo[0:COUT] = (by_x - x_high.astype(F32)).astype(BF16)
    rlo[COUT:] = (by_up - up_high.astype(F32)).astype(BF16)
    shift = base[...] - all_mean[:, :COUT]
    from_up = exact(all_mean[:, COUT:], by_up)
    level = exact(shift, by_x) - from_up
    mix[0:COUT] = by_x[:, COUT:]
    mix[COUT : 2 * COUT] = by_up[:, COUT:]
    mix[2 * COUT :] = -exact(all_mean[:, :COUT], by_x[:, COUT:]) - from_up[:, COUT:]
    consts[:, :COUT] = level[:, :COUT] + offset[...]
    consts[:, COUT:] = level[:, COUT:]

    def spread(block):
        return jnp.concatenate(
            [from_right(block).astype(BF16), block.astype(BF16), from_left(block).astype(BF16)],
            axis=1,
        )

    def finish(lhs):
        out = fast(lhs, rhi[...]) + fast(lhs[:, COUT:], rlo[...]) + consts[0:1, :]
        return out[:, :COUT].astype(BF16), spread(out[:, COUT:])

    def pg_up(b):
        return remote(
            pg3.at[b, 1, :, pl.ds(COUT, COUT)],
            pg_halo.at[1, b],
            pg_send.at[0, b],
            pg_recv.at[0, b],
            up_device,
        )

    def pg_down(b):
        return remote(
            pg3.at[b, BAND, :, pl.ds(COUT, COUT)],
            pg_halo.at[0, b],
            pg_send.at[1, b],
            pg_recv.at[1, b],
            down_device,
        )

    @pl.loop(0, IMGS)
    def _(b):
        shown, grads = finish(jnp.concatenate([x3[b, 0], x3[b, BAND - 1]], axis=0))
        colored[b, 0] = shown[:WID]
        colored[b, BAND - 1] = shown[WID:]
        pg3[b, 1] = grads[:WID]
        pg3[b, BAND] = grads[WID:]

        @pl.when(has_up)
        def _():
            pg_up(b).start()

        @pl.when(has_down)
        def _():
            pg_down(b).start()

    step(1, 4)
    step(2, 3)

    @pl.loop(0, IMGS)
    def _(b):
        shown, grads = finish(x3[b, pl.ds(1, inner)].reshape(inner * WID, 3 * COUT))
        colored[b, pl.ds(1, inner)] = shown.reshape(inner, WID, COUT)
        pg3[b, pl.ds(2, inner)] = grads.reshape(inner, WID, ONE_ROW)

    color_grad[0] = s0 * (1.0 / math.sqrt(total_pix))
    color_grad[1] = s1 * (1.0 / math.sqrt(total_pix))

    def image_grad(b):
        lhs = jnp.concatenate(
            [pg3[b, pl.ds(2 - a, BAND)].reshape(BAND * WID, ONE_ROW) for a in range(3)],
            axis=1,
        )
        grad_images[b] = fast(lhs, wb[...]).astype(BF16).reshape(BAND, WID, CIN)

    step(0, 4)
    step(1, 5)
    step(2, 4)

    @pl.loop(0, IMGS)
    def _(b):
        @pl.when(has_down)
        def _():
            pg_up(b).wait_recv()
            pg3[b, BAND + 1] = spread(pg_halo[1, b].astype(F32))

        @pl.when(has_up)
        def _():
            pg_down(b).wait_recv()
            pg3[b, 0] = spread(pg_halo[0, b].astype(F32))

    image_grad(0)
    image_grad(1)
    step(0, 5)
    image_grad(2)
    step(1, 6)
    image_grad(3)
    step(2, 5)
    step(1, 7)
    image_grad(4)
    step(0, 6)
    image_grad(5)
    step(0, 7)
    step(2, 6)
    step(2, 7)

    @pl.loop(0, IMGS)
    def _(b):
        @pl.when(has_up)
        def _():
            halo_up(b).wait_send()
            pg_up(b).wait_send()

        @pl.when(has_down)
        def _():
            halo_down(b).wait_send()
            pg_down(b).wait_send()


def place_kernel(*refs):
    count = (len(refs) - 1) // 2
    copies = [
        pltpu.make_async_copy(refs[i], refs[count + i], refs[-1].at[i]) for i in range(count)
    ]
    for copy in copies:
        copy.start()
    for copy in copies:
        copy.wait()


def body(images, kernel, colors, offset, upstream):
    total_pix = PIX * lax.axis_size("dp") * lax.axis_size("rows")
    anywhere = pl.BlockSpec(memory_space=pl.ANY)
    outside = pl.BlockSpec(memory_space=pltpu.HBM)
    local = pl.BlockSpec(memory_space=pltpu.VMEM)
    dma = pltpu.SemaphoreType.DMA
    shapes = (
        jax.ShapeDtypeStruct((IMGS, BAND, WID, COUT), BF16),
        jax.ShapeDtypeStruct((IMGS, BAND, WID, CIN), BF16),
        jax.ShapeDtypeStruct((3, 3, CIN, COUT), F32),
        jax.ShapeDtypeStruct((2, GS, GS), F32),
    )
    results = pl.pallas_call(
        functools.partial(block_kernel, total_pix),
        out_shape=shapes,
        in_specs=[outside] * 5,
        out_specs=(local, local, local, local),
        scratch_shapes=[
            pltpu.VMEM((IMGS, BAND + 2, WID, CIN), BF16),
            pltpu.VMEM((IMGS, BAND, WID, 3 * COUT), BF16),
            pltpu.VMEM((3 * CIN, ONE_ROW), BF16),
            pltpu.VMEM((3 * ONE_ROW, CIN), BF16),
            pltpu.VMEM((2, GS, GS), F32),
            pltpu.VMEM((1, COUT), F32),
            pltpu.VMEM((IMGS, BAND + 2, 3 * CIN, WID), BF16),
            pltpu.VMEM((BAND + 2, 3, 8, CIN), F32),
            pltpu.VMEM((3, 3 * CIN, COUT), F32),
            pltpu.VMEM((IMGS, BAND + 2, WID, ONE_ROW), BF16),
            pltpu.VMEM((2, IMGS, WID, COUT), BF16),
            pltpu.VMEM((8, COUT), F32),
            pltpu.VMEM((8, 2 * COUT), F32),
            pltpu.VMEM((COUT, 2 * COUT), F32),
            pltpu.VMEM((3 * COUT, 2 * COUT), BF16),
            pltpu.VMEM((2 * COUT, 2 * COUT), BF16),
            pltpu.VMEM((2 * COUT + 8, COUT), F32),
            pltpu.VMEM((8, 2 * COUT), F32),
            pltpu.VMEM((OCT, 16, 2 * COUT), F32),
            pltpu.VMEM((OCT, 16, 2 * COUT), F32),
            pltpu.VMEM((PLANE, 16, 2 * COUT), F32),
            pltpu.VMEM((OCT, 16, 2 * COUT), F32),
            pltpu.VMEM((OCT, 8, 2 * COUT), F32),
            pltpu.VMEM((3, 3 * CIN, 2 * COUT), F32),
            pltpu.VMEM((3, 3 * CIN // 2, 2 * COUT), F32),
            pltpu.VMEM((3, RING - 1, 3 * CIN // 8, 2 * COUT), F32),
            pltpu.VMEM((3, 3 * CIN // 8, 2 * COUT), F32),
            pltpu.VMEM((3, RING - 1, 3 * CIN // 32, 2 * COUT), F32),
            pltpu.VMEM((3, RING, 3 * CIN // 32, 2 * COUT), F32),
            pltpu.VMEM((3, 3 * CIN, COUT), F32),
            dma((IMGS + 1,)),
            dma((11,)),
            dma((2, IMGS)),
            dma((2, IMGS)),
            dma((OCT - 1,)),
            dma((OCT - 1,)),
            dma((PLANE - 1,)),
            dma((PLANE - 1,)),
            dma((OCT - 1,)),
            dma((OCT - 1,)),
            dma((2, IMGS)),
            dma((2, IMGS)),
            dma((3, 2)),
            dma((3, 2)),
            dma((3, 5, RING - 1)),
            dma((3, 5, RING - 1)),
        ],
        compiler_params=pltpu.CompilerParams(
            collective_id=0, has_side_effects=True, vmem_limit_bytes=44 * 1024 * 1024
        ),
    )(
        *[
            pltpu.with_memory_space_constraint(given, pltpu.HBM)
            for given in (images, kernel, colors, offset.reshape(1, COUT), upstream)
        ]
    )
    return pl.pallas_call(
        place_kernel,
        out_shape=shapes,
        in_specs=[anywhere] * 4,
        out_specs=(anywhere,) * 4,
        scratch_shapes=[dma((4,))],
        compiler_params=pltpu.CompilerParams(vmem_limit_bytes=1024 * 1024),
    )(*results)


def solution(mesh):
    placed = (P("dp", "rows", None, None), P(), P(), P(), P("dp", "rows", None, None))
    return jax.shard_map(
        body,
        mesh=mesh,
        in_specs=placed,
        out_specs=(P("dp", "rows", None, None), P("dp", "rows", None, None), P(), P()),
        check_vma=False,
    )
```

```python
import functools
import math

import jax
import jax.numpy as jnp
from jax import lax
from jax.experimental import pallas as pl
from jax.experimental.pallas import tpu as pltpu
from jax.sharding import PartitionSpec as P

NS_ITERS = 5
EPSILON = 1e-05
PRECISE = lax.Precision.HIGHEST
BF16 = jnp.bfloat16
F32 = jnp.float32
MESH = pl.DeviceIdType.MESH

IMGS, BAND, WID, CIN, COUT, GS = 6, 8, 128, 256, 128, 64
RING = 4
OCT = 8
PLANE = 16
PIX = IMGS * BAND * WID
ONE_ROW = COUT * 3


def exact(left, right, dims=((1,), (0,))):
    return lax.dot_general(
        left, right, (dims, ((), ())), precision=PRECISE, preferred_element_type=F32
    )


def fast(left, right):
    return jnp.dot(left, right, preferred_element_type=F32)


def from_left(block):
    place = lax.broadcasted_iota(jnp.int32, block.shape, 0) % WID
    return jnp.where(place == 0, 0.0, pltpu.roll(block, 1, 0))


def from_right(block):
    place = lax.broadcasted_iota(jnp.int32, block.shape, 0) % WID
    return jnp.where(place == WID - 1, 0.0, pltpu.roll(block, block.shape[0] - 1, 0))


def pack(full):
    lane = lax.broadcasted_iota(jnp.int32, (GS, full.shape[1]), 1) % COUT
    return jnp.where(lane < GS, full[:GS], full[GS:])


def upper(top):
    lane = lax.broadcasted_iota(jnp.int32, top.shape, 1)
    return jnp.concatenate([top, jnp.where(lane < GS, 0.0, pltpu.roll(top, GS, 1))], axis=0)


def diag_pair(first, second):
    zero = jnp.zeros((GS, GS), F32)
    return jnp.concatenate(
        [
            jnp.concatenate([first, zero], axis=1),
            jnp.concatenate([zero, second], axis=1),
        ],
        axis=0,
    )


def whiten_terms(packed, colors, total_pix, between):
    row = lax.broadcasted_iota(jnp.int32, (GS, GS), 0)
    col = lax.broadcasted_iota(jnp.int32, (GS, GS), 1)
    eye = jnp.where(row == col, 1.0, 0.0).astype(F32)
    cross = packed[:, COUT:].T
    tops, fulls, traces, crosses = [], [], [], []
    for group in range(2):
        sigma = packed[:, group * GS : (group + 1) * GS] * (1.0 / total_pix) + EPSILON * eye
        trace = jnp.sum(jnp.sum(sigma * eye, axis=1, keepdims=True), axis=0, keepdims=True)
        along = cross[group * GS : (group + 1) * GS]
        grad = exact(colors[group].T, along)
        tops.append(jnp.concatenate([sigma / trace, grad], axis=1))
        fulls.append(upper(tops[-1]))
        traces.append(trace)
        crosses.append(along)
    wide_eye = jnp.concatenate([eye, jnp.zeros((GS, GS), F32)], axis=1)
    states = [1.5 * wide_eye - 0.5 * top for top in tops]
    for repeat in range(NS_ITERS - 1):
        if repeat == 2:
            between()
        squares = [exact(state, upper(state)) for state in states]
        by_normed = [exact(state, full) for state, full in zip(states, fulls)]
        cubes = [exact(square, upper(term)) for square, term in zip(squares, by_normed)]
        states = [1.5 * state - 0.5 * cube for state, cube in zip(states, cubes)]
    found = []
    for group in range(2):
        trace = traces[group]
        root = lax.rsqrt(trace)
        estimate, slope = states[group][:, :GS], states[group][:, GS:]
        normed, grad = tops[group][:, :GS], tops[group][:, GS:]
        scalar = slope * normed + 0.5 * grad * estimate
        scalar = jnp.sum(jnp.sum(scalar, axis=1, keepdims=True), axis=0, keepdims=True)
        sigma_grad = (slope - eye * scalar) * (root / trace)
        both = (sigma_grad + sigma_grad.T) * (1.0 / total_pix)
        whitener = estimate * root
        colored_by = exact(colors[group], whitener)
        color_sum = exact(crosses[group], whitener, ((1,), (1,)))
        found.append((colored_by, both, color_sum))
    return found


def block_kernel(
    total_pix,
    images,
    kernel,
    colors_in,
    offset_in,
    upstream,
    colored,
    grad_images,
    kernel_grad,
    color_grad,
    img,
    x3,
    wf,
    wb,
    colors,
    offset,
    imgt,
    window,
    window_col,
    pg3,
    pg_halo,
    base,
    sums,
    moments,
    rhi,
    rlo,
    mix,
    consts,
    stat_src,
    stat_a,
    stat_p,
    stat_all,
    spare,
    gk,
    rx_core,
    rx_first,
    held,
    rx_second,
    rx_third,
    full,
    shared,
    load_sem,
    weight_sem,
    halo_send,
    halo_recv,
    oct_send,
    oct_recv,
    plane_send,
    plane_recv,
    back_send,
    back_recv,
    pg_send,
    pg_recv,
    gk_core_send,
    gk_core_recv,
    gk_line_send,
    gk_line_recv,
):
    dp = lax.axis_index("dp")
    y = lax.axis_index("rows")
    x = dp // (RING * 2)
    z = (dp // 2) % RING
    core = dp % 2
    octet = x * 2 + core
    spot = y * RING + z
    inner = BAND - 2
    has_up = y > 0
    has_down = y < RING - 1

    def remote(src, dst, send, recv, device):
        return pltpu.make_async_remote_copy(
            src_ref=src,
            dst_ref=dst,
            send_sem=send,
            recv_sem=recv,
            device_id=device,
            device_id_type=MESH,
        )

    def oct_device(index):
        return (((index // 2) * RING + z) * 2 + index % 2, y)

    def plane_device(index):
        return ((x * RING + index % RING) * 2 + core, index // RING)

    up_device = (dp, (y + RING - 1) % RING)
    down_device = (dp, (y + 1) % RING)
    other_core = (dp + 1 - 2 * core, y)

    weight_loads = [
        pltpu.make_async_copy(
            kernel.at[a, c],
            wf.at[pl.ds(a * CIN, CIN), pl.ds(c * COUT, COUT)],
            weight_sem.at[a * 3 + c],
        )
        for a in range(3)
        for c in range(3)
    ] + [
        pltpu.make_async_copy(colors_in, colors, weight_sem.at[9]),
        pltpu.make_async_copy(offset_in, offset, weight_sem.at[10]),
    ]

    def load(b):
        return pltpu.make_async_copy(images.at[b], img.at[b, pl.ds(1, BAND)], load_sem.at[b])

    up_load = pltpu.make_async_copy(
        upstream, x3.at[:, :, :, pl.ds(2 * COUT, COUT)], load_sem.at[IMGS]
    )

    barrier = pltpu.get_barrier_semaphore()
    for k in range(1, PLANE):
        pl.semaphore_signal(
            barrier, inc=1, device_id=plane_device((spot + k) % PLANE), device_id_type=MESH
        )
    for k in range(1, OCT):
        pl.semaphore_signal(
            barrier, inc=1, device_id=oct_device((octet + k) % OCT), device_id_type=MESH
        )
    for copy in weight_loads:
        copy.start()
    for b in range(IMGS):
        load(b).start()
    up_load.start()

    @pl.when(y == 0)
    def _():
        img[:, 0] = jnp.zeros((IMGS, WID, CIN), BF16)
        pg3[:, 0] = jnp.zeros((IMGS, WID, ONE_ROW), BF16)

    @pl.when(y == RING - 1)
    def _():
        img[:, BAND + 1] = jnp.zeros((IMGS, WID, CIN), BF16)
        pg3[:, BAND + 1] = jnp.zeros((IMGS, WID, ONE_ROW), BF16)

    sums[...] = jnp.zeros_like(sums)
    moments[...] = jnp.zeros_like(moments)
    pl.semaphore_wait(barrier, OCT - 1 + PLANE - 1)

    def halo_up(b):
        return remote(
            images.at[b, 0],
            img.at[b, BAND + 1],
            halo_send.at[0, b],
            halo_recv.at[0, b],
            up_device,
        )

    def halo_down(b):
        return remote(
            images.at[b, BAND - 1],
            img.at[b, 0],
            halo_send.at[1, b],
            halo_recv.at[1, b],
            down_device,
        )

    for b in range(IMGS):

        @pl.when(has_up)
        def _():
            halo_up(b).start()

        @pl.when(has_down)
        def _():
            halo_down(b).start()

    for copy in weight_loads:
        copy.wait()
    up_load.wait()

    def conv(lhs):
        out = fast(lhs, wf[...])
        return (
            from_left(out[:, :COUT])
            + out[:, COUT : 2 * COUT]
            + from_right(out[:, 2 * COUT :])
        )

    def absorb(block, ups):
        apart = block - base[0:1, :]
        high = apart.astype(BF16)
        low = (apart - high.astype(F32)).astype(BF16)
        sums[:, :COUT] = sums[:, :COUT] + apart.reshape(-1, 8, COUT).sum(axis=0)
        sums[:, COUT:] = sums[:, COUT:] + ups.astype(F32).reshape(-1, 8, COUT).sum(axis=0)
        moments[...] = moments[...] + fast(high.T, jnp.concatenate([high, ups], axis=1))
        return jnp.concatenate([low, high], axis=1)

    def inner_conv(b):
        load(b).wait()
        return conv(
            jnp.concatenate(
                [img[b, pl.ds(1 + a, inner)].reshape(inner * WID, CIN) for a in range(3)],
                axis=1,
            )
        )

    def inner_absorb(b, block):
        ups = x3[b, pl.ds(1, inner), :, 2 * COUT :].reshape(inner * WID, COUT)
        both = absorb(block, ups)
        x3[b, pl.ds(1, inner), :, : 2 * COUT] = both.reshape(inner, WID, 2 * COUT)

    first = inner_conv(0)
    base[...] = jnp.broadcast_to(
        jnp.sum(first, axis=0, keepdims=True) * (1.0 / (inner * WID)), (8, COUT)
    )
    inner_absorb(0, first)

    @pl.loop(1, IMGS)
    def _(b):
        inner_absorb(b, inner_conv(b))

    for a in range(3):
        for c in range(3):
            tap = wf[a * CIN : (a + 1) * CIN, c * COUT : (c + 1) * COUT]
            wb[a * ONE_ROW + c * COUT : a * ONE_ROW + (c + 1) * COUT, :] = tap.T
    window[...] = jnp.zeros_like(window)

    def turn(b, row):
        values = img[b, row].astype(F32)
        for c, moved in enumerate((from_left(values), values, from_right(values))):
            imgt[b, row, c * CIN : (c + 1) * CIN, :] = moved.astype(BF16).T

    lane_row = lax.broadcasted_iota(jnp.int32, (8, CIN), 0)

    def count(b, row):
        values = img[b, row].astype(F32)
        total = values.reshape(-1, 8, CIN).sum(axis=0)
        window[row, 0] = window[row, 0] + (
            total - jnp.where(lane_row == 7, values[WID - 8 :], 0.0)
        )
        window[row, 1] = window[row, 1] + total
        window[row, 2] = window[row, 2] + (total - jnp.where(lane_row == 0, values[:8], 0.0))

    @pl.loop(0, IMGS)
    def _(b):
        for row in range(1, BAND + 1):
            count(b, row)

    @pl.loop(0, IMGS)
    def _(b):
        @pl.when(has_down)
        def _():
            halo_up(b).wait_recv()

        @pl.when(has_up)
        def _():
            halo_down(b).wait_recv()

        block = conv(
            jnp.concatenate(
                [
                    jnp.concatenate([img[b, a], img[b, BAND - 1 + a]], axis=0)
                    for a in range(3)
                ],
                axis=1,
            )
        )
        ups = jnp.concatenate(
            [x3[b, 0, :, 2 * COUT :], x3[b, BAND - 1, :, 2 * COUT :]], axis=0
        )
        both = absorb(block, ups)
        x3[b, 0, :, : 2 * COUT] = both[:WID]
        x3[b, BAND - 1, :, : 2 * COUT] = both[WID:]
        count(b, 0)
        count(b, BAND + 1)

    orders = (("z", "x", "y"), ("x", "y", "z"), ("y", "z", "x"))
    where = {"x": x, "y": y, "z": z}
    half = 3 * CIN // 2
    quarter = half // RING
    piece = quarter // RING

    def rows_at(start, size):
        return pl.ds(pl.multiple_of(start, 32 if size % 32 == 0 else 8), size)

    def axis_device(axis, index):
        if axis == "x":
            return oct_device(index * 2 + core)
        return plane_device(index * RING + z if axis == "y" else y * RING + index)

    mine = rows_at(core * half, half)
    theirs = rows_at((1 - core) * half, half)
    flying = {}

    def start(part, copies):
        for copy in copies:
            copy.start()
        flying[part] = copies

    def settle(part):
        for copy in flying[part]:
            copy.wait()

    def line_copies(part, stage, src, dst):
        axis = orders[part][(0, 1, 2, 1, 0)[stage]]
        me = where[axis]
        return [
            remote(
                src((me + k) % RING),
                dst(k),
                gk_line_send.at[part, stage, k - 1],
                gk_line_recv.at[part, stage, k - 1],
                axis_device(axis, (me + k) % RING),
            )
            for k in range(1, RING)
        ]

    def step(part, stage):
        first, second, third = (where[axis] for axis in orders[part])
        my_quarter = rows_at(core * half + first * quarter, quarter)
        my_piece = rows_at(core * half + first * quarter + second * piece, piece)
        if stage > 0:
            settle(part)
        if stage == 0:
            start(
                part,
                [
                    remote(
                        gk.at[part, theirs],
                        rx_core.at[part],
                        gk_core_send.at[part, 0],
                        gk_core_recv.at[part, 0],
                        other_core,
                    )
                ],
            )
        elif stage == 1:
            gk[part, mine] = gk[part, mine] + rx_core[part]
            start(
                part,
                line_copies(
                    part,
                    0,
                    lambda index: gk.at[part, rows_at(core * half + index * quarter, quarter)],
                    lambda k: rx_first.at[part, k - 1],
                ),
            )
        elif stage == 2:
            held[part] = (
                (gk[part, my_quarter] + rx_first[part, 0])
                + (rx_first[part, 1] + rx_first[part, 2])
            )
            start(
                part,
                line_copies(
                    part,
                    1,
                    lambda index: held.at[part, rows_at(index * piece, piece)],
                    lambda k: rx_second.at[part, k - 1],
                ),
            )
        elif stage == 3:
            rx_third[part, third] = (
                (held[part, rows_at(second * piece, piece)] + rx_second[part, 0])
                + (rx_second[part, 1] + rx_second[part, 2])
            )
            start(
                part,
                line_copies(
                    part,
                    2,
                    lambda index: rx_third.at[part, third],
                    lambda k: rx_third.at[part, third],
                ),
            )
        elif stage == 4:
            total = (rx_third[part, 0] + rx_third[part, 1]) + (
                rx_third[part, 2] + rx_third[part, 3]
            )
            full[part, my_piece] = (
                exact(total, mix[0 : 2 * COUT])
                + window_col[part, my_piece] * mix[2 * COUT : 2 * COUT + 1]
            )
            start(
                part,
                line_copies(
                    part,
                    3,
                    lambda index: full.at[part, my_piece],
                    lambda k: full.at[part, my_piece],
                ),
            )
        elif stage == 5:
            shared[part, my_quarter] = full[part, my_quarter].astype(BF16)
            start(
                part,
                line_copies(
                    part,
                    4,
                    lambda index: shared.at[part, my_quarter],
                    lambda k: shared.at[part, my_quarter],
                ),
            )
        elif stage == 6:
            start(
                part,
                [
                    remote(
                        shared.at[part, mine],
                        shared.at[part, mine],
                        gk_core_send.at[part, 1],
                        gk_core_recv.at[part, 1],
                        other_core,
                    )
                ],
            )
        elif stage == 7:
            for c in range(3):
                kernel_grad[part, c] = shared[part, c * CIN : (c + 1) * CIN].astype(F32) * (
                    1.0 / math.sqrt(total_pix)
                )

    own = jnp.sum(sums[...], axis=0, keepdims=True) * (1.0 / PIX)
    drift = own[:, :COUT]
    column = jnp.broadcast_to(drift, (COUT, COUT)).T
    packed = pack(
        moments[...] - float(PIX) * jnp.concatenate([column, column], axis=1) * own
    )
    own_mean = jnp.concatenate([drift + base[0:1, :], own[:, COUT:]], axis=1)
    index = lax.broadcasted_iota(jnp.int32, (8, 2 * COUT), 0)
    taps = []
    for a in range(3):
        for c in range(3):
            total = window[a, c]
            for row in range(a + 1, a + BAND):
                total = total + window[row, c]
            taps.append(jnp.sum(total, axis=0, keepdims=True))
    taps = taps + [jnp.zeros_like(taps[0])] * (2 * OCT - len(taps))
    for slot in range(OCT):
        stat_src[slot, 0:8] = packed[slot * 8 : slot * 8 + 8]
        tail = jnp.where(index == 0, own_mean, 0.0)
        tail = jnp.where(index == 1, taps[2 * slot], tail)
        stat_src[slot, 8:16] = jnp.where(index == 2, taps[2 * slot + 1], tail)

    def columns_of(rows):
        place = lax.broadcasted_iota(jnp.int32, (2 * OCT, CIN), 0)
        stacked = jnp.zeros((2 * OCT, CIN), F32)
        for tap in range(9):
            stacked = jnp.where(place == tap, rows[tap], stacked)
        return stacked.T

    round_one = []
    for k in range(1, OCT):
        target = (octet + k) % OCT
        round_one.append(
            remote(
                stat_src.at[target],
                stat_a.at[octet],
                oct_send.at[k - 1],
                oct_recv.at[k - 1],
                oct_device(target),
            )
        )
    for copy in round_one:
        copy.start()
    stat_a[octet] = stat_src[octet]

    own_cols = columns_of(taps)

    def weight_part(a):
        lhs = jnp.concatenate([imgt[b, a + h] for b in range(IMGS) for h in range(BAND)], axis=1)
        gk[a] = fast(lhs, x3[:, :, :, COUT:].reshape(PIX, 2 * COUT))
        for c in range(3):
            column = own_cols[:, a * 3 + c : a * 3 + c + 1]
            rows = slice(c * CIN, (c + 1) * CIN)
            gk[a, rows, :COUT] = gk[a, rows, :COUT] + column * base[0:1, :]

    @pl.loop(0, IMGS)
    def _(b):
        for row in range(BAND + 2):
            turn(b, row)

    for copy in round_one:
        copy.wait()

    def spread_of(means, pixels):
        middle = jnp.sum(means, axis=0, keepdims=True) * (1.0 / means.shape[0])
        apart = means - middle
        return middle, pack(exact(apart[:, :COUT].T, apart)) * float(pixels)

    def tails_of(buf, count):
        place = lax.broadcasted_iota(jnp.int32, (count, 2 * COUT), 0)
        rows, tail = buf[0, 0:8], buf[0, 8:16]
        means = jnp.broadcast_to(buf[0, 8:9], (count, 2 * COUT))
        for slot in range(1, count):
            rows = rows + buf[slot, 0:8]
            tail = tail + buf[slot, 8:16]
            means = jnp.where(place == slot, buf[slot, 8:9], means)
        return rows, tail, means

    rows, tail, means = tails_of(stat_a, OCT)
    middle, between = spread_of(means, PIX)
    for slot in range(OCT):
        spare[slot] = between[slot * 8 : slot * 8 + 8]
    stat_p[spot, 0:8] = rows + spare[octet]
    stat_p[spot, 8:16] = jnp.where(index == 0, middle, tail)
    round_two = [
        remote(
            stat_p.at[spot],
            stat_p.at[spot],
            plane_send.at[k - 1],
            plane_recv.at[k - 1],
            plane_device((spot + k) % PLANE),
        )
        for k in range(1, PLANE)
    ]
    for copy in round_two:
        copy.start()
    weight_part(1)
    step(1, 0)
    weight_part(0)
    step(0, 0)
    step(1, 1)
    weight_part(2)
    step(2, 0)
    for copy in round_two:
        copy.wait()
    rows, tail, means = tails_of(stat_p, PLANE)
    stat_all[octet, 0:8] = rows
    stat_all[octet, 8:16] = tail
    round_three = [
        remote(
            stat_all.at[octet],
            stat_all.at[octet],
            back_send.at[k - 1],
            back_recv.at[k - 1],
            oct_device((octet + k) % OCT),
        )
        for k in range(1, OCT)
    ]
    for copy in round_three:
        copy.start()
    step(0, 1)
    step(2, 1)
    middle, between = spread_of(means, PIX * OCT)
    all_mean = jnp.broadcast_to(middle, (8, 2 * COUT))
    step(1, 2)
    for copy in round_three:
        copy.wait()
    packed = jnp.concatenate([stat_all[slot, 0:8] for slot in range(OCT)], axis=0) + between
    all_cols = columns_of([stat_all[tap // 2, 9 + tap % 2 : 10 + tap % 2] for tap in range(9)])
    for a in range(3):
        for c in range(3):
            window_col[a, c * CIN : (c + 1) * CIN, :] = jnp.broadcast_to(
                all_cols[:, a * 3 + c : a * 3 + c + 1], (CIN, COUT)
            )

    (t0, b0, s0), (t1, b1, s1) = whiten_terms(
        packed, colors, total_pix, lambda: (step(0, 2), step(2, 2))
    )
    by_x = jnp.concatenate([diag_pair(t0.T, t1.T), diag_pair(b0, b1)], axis=1)
    by_up = jnp.concatenate([jnp.zeros((COUT, COUT), F32), diag_pair(t0, t1)], axis=1)
    x_high, up_high = by_x.astype(BF16), by_up.astype(BF16)
    rhi[0:COUT] = x_high
    rhi[COUT : 2 * COUT] = x_high
    rhi[2 * COUT :] = up_high
    rlo[0:COUT] = (by_x - x_high.astype(F32)).astype(BF16)
    rlo[COUT:] = (by_up - up_high.astype(F32)).astype(BF16)
    shift = base[...] - all_mean[:, :COUT]
    from_up = exact(all_mean[:, COUT:], by_up)
    level = exact(shift, by_x) - from_up
    mix[0:COUT] = by_x[:, COUT:]
    mix[COUT : 2 * COUT] = by_up[:, COUT:]
    mix[2 * COUT :] = -exact(all_mean[:, :COUT], by_x[:, COUT:]) - from_up[:, COUT:]
    consts[:, :COUT] = level[:, :COUT] + offset[...]
    consts[:, COUT:] = level[:, COUT:]

    step(1, 3)

    def spread(block):
        return jnp.concatenate(
            [from_right(block).astype(BF16), block.astype(BF16), from_left(block).astype(BF16)],
            axis=1,
        )

    def finish(lhs):
        out = fast(lhs, rhi[...]) + fast(lhs[:, COUT:], rlo[...]) + consts[0:1, :]
        return out[:, :COUT].astype(BF16), spread(out[:, COUT:])

    def pg_up(b):
        return remote(
            pg3.at[b, 1, :, pl.ds(COUT, COUT)],
            pg_halo.at[1, b],
            pg_send.at[0, b],
            pg_recv.at[0, b],
            up_device,
        )

    def pg_down(b):
        return remote(
            pg3.at[b, BAND, :, pl.ds(COUT, COUT)],
            pg_halo.at[0, b],
            pg_send.at[1, b],
            pg_recv.at[1, b],
            down_device,
        )

    @pl.loop(0, IMGS)
    def _(b):
        shown, grads = finish(jnp.concatenate([x3[b, 0], x3[b, BAND - 1]], axis=0))
        colored[b, 0] = shown[:WID]
        colored[b, BAND - 1] = shown[WID:]
        pg3[b, 1] = grads[:WID]
        pg3[b, BAND] = grads[WID:]

        @pl.when(has_up)
        def _():
            pg_up(b).start()

        @pl.when(has_down)
        def _():
            pg_down(b).start()

    def inner_finish(b):
        shown, grads = finish(x3[b, pl.ds(1, inner)].reshape(inner * WID, 3 * COUT))
        colored[b, pl.ds(1, inner)] = shown.reshape(inner, WID, COUT)
        pg3[b, pl.ds(2, inner)] = grads.reshape(inner, WID, ONE_ROW)

    pl.loop(0, IMGS // 2)(inner_finish)
    step(0, 3)
    step(2, 3)
    pl.loop(IMGS // 2, IMGS)(inner_finish)
    color_grad[0] = s0 * (1.0 / math.sqrt(total_pix))
    color_grad[1] = s1 * (1.0 / math.sqrt(total_pix))

    def image_grad(b):
        lhs = jnp.concatenate(
            [pg3[b, pl.ds(2 - a, BAND)].reshape(BAND * WID, ONE_ROW) for a in range(3)],
            axis=1,
        )
        grad_images[b] = fast(lhs, wb[...]).astype(BF16).reshape(BAND, WID, CIN)

    step(1, 4)

    @pl.loop(0, IMGS)
    def _(b):
        @pl.when(has_down)
        def _():
            pg_up(b).wait_recv()
            pg3[b, BAND + 1] = spread(pg_halo[1, b].astype(F32))

        @pl.when(has_up)
        def _():
            pg_down(b).wait_recv()
            pg3[b, 0] = spread(pg_halo[0, b].astype(F32))

    image_grad(0)
    image_grad(1)
    step(0, 4)
    step(2, 4)
    image_grad(2)
    step(1, 5)
    image_grad(3)
    image_grad(4)
    step(0, 5)
    step(2, 5)
    image_grad(5)
    step(1, 6)
    step(1, 7)
    step(0, 6)
    step(2, 6)
    step(0, 7)
    step(2, 7)

    @pl.loop(0, IMGS)
    def _(b):
        @pl.when(has_up)
        def _():
            halo_up(b).wait_send()
            pg_up(b).wait_send()

        @pl.when(has_down)
        def _():
            halo_down(b).wait_send()
            pg_down(b).wait_send()


def place_kernel(*refs):
    count = (len(refs) - 1) // 2
    copies = [
        pltpu.make_async_copy(refs[i], refs[count + i], refs[-1].at[i]) for i in range(count)
    ]
    for copy in copies:
        copy.start()
    for copy in copies:
        copy.wait()


def body(images, kernel, colors, offset, upstream):
    total_pix = PIX * lax.axis_size("dp") * lax.axis_size("rows")
    anywhere = pl.BlockSpec(memory_space=pl.ANY)
    outside = pl.BlockSpec(memory_space=pltpu.HBM)
    local = pl.BlockSpec(memory_space=pltpu.VMEM)
    dma = pltpu.SemaphoreType.DMA
    shapes = (
        jax.ShapeDtypeStruct((IMGS, BAND, WID, COUT), BF16),
        jax.ShapeDtypeStruct((IMGS, BAND, WID, CIN), BF16),
        jax.ShapeDtypeStruct((3, 3, CIN, COUT), F32),
        jax.ShapeDtypeStruct((2, GS, GS), F32),
    )
    results = pl.pallas_call(
        functools.partial(block_kernel, total_pix),
        out_shape=shapes,
        in_specs=[outside] * 5,
        out_specs=(local, local, local, local),
        scratch_shapes=[
            pltpu.VMEM((IMGS, BAND + 2, WID, CIN), BF16),
            pltpu.VMEM((IMGS, BAND, WID, 3 * COUT), BF16),
            pltpu.VMEM((3 * CIN, ONE_ROW), BF16),
            pltpu.VMEM((3 * ONE_ROW, CIN), BF16),
            pltpu.VMEM((2, GS, GS), F32),
            pltpu.VMEM((1, COUT), F32),
            pltpu.VMEM((IMGS, BAND + 2, 3 * CIN, WID), BF16),
            pltpu.VMEM((BAND + 2, 3, 8, CIN), F32),
            pltpu.VMEM((3, 3 * CIN, COUT), F32),
            pltpu.VMEM((IMGS, BAND + 2, WID, ONE_ROW), BF16),
            pltpu.VMEM((2, IMGS, WID, COUT), BF16),
            pltpu.VMEM((8, COUT), F32),
            pltpu.VMEM((8, 2 * COUT), F32),
            pltpu.VMEM((COUT, 2 * COUT), F32),
            pltpu.VMEM((3 * COUT, 2 * COUT), BF16),
            pltpu.VMEM((2 * COUT, 2 * COUT), BF16),
            pltpu.VMEM((2 * COUT + 8, COUT), F32),
            pltpu.VMEM((8, 2 * COUT), F32),
            pltpu.VMEM((OCT, 16, 2 * COUT), F32),
            pltpu.VMEM((OCT, 16, 2 * COUT), F32),
            pltpu.VMEM((PLANE, 16, 2 * COUT), F32),
            pltpu.VMEM((OCT, 16, 2 * COUT), F32),
            pltpu.VMEM((OCT, 8, 2 * COUT), F32),
            pltpu.VMEM((3, 3 * CIN, 2 * COUT), F32),
            pltpu.VMEM((3, 3 * CIN // 2, 2 * COUT), F32),
            pltpu.VMEM((3, RING - 1, 3 * CIN // 8, 2 * COUT), F32),
            pltpu.VMEM((3, 3 * CIN // 8, 2 * COUT), F32),
            pltpu.VMEM((3, RING - 1, 3 * CIN // 32, 2 * COUT), F32),
            pltpu.VMEM((3, RING, 3 * CIN // 32, 2 * COUT), F32),
            pltpu.VMEM((3, 3 * CIN, COUT), F32),
            pltpu.VMEM((3, 3 * CIN, COUT), BF16),
            dma((IMGS + 1,)),
            dma((11,)),
            dma((2, IMGS)),
            dma((2, IMGS)),
            dma((OCT - 1,)),
            dma((OCT - 1,)),
            dma((PLANE - 1,)),
            dma((PLANE - 1,)),
            dma((OCT - 1,)),
            dma((OCT - 1,)),
            dma((2, IMGS)),
            dma((2, IMGS)),
            dma((3, 2)),
            dma((3, 2)),
            dma((3, 5, RING - 1)),
            dma((3, 5, RING - 1)),
        ],
        compiler_params=pltpu.CompilerParams(
            collective_id=0, has_side_effects=True, vmem_limit_bytes=44 * 1024 * 1024
        ),
    )(
        *[
            pltpu.with_memory_space_constraint(given, pltpu.HBM)
            for given in (images, kernel, colors, offset.reshape(1, COUT), upstream)
        ]
    )
    return pl.pallas_call(
        place_kernel,
        out_shape=shapes,
        in_specs=[anywhere] * 4,
        out_specs=(anywhere,) * 4,
        scratch_shapes=[dma((4,))],
        compiler_params=pltpu.CompilerParams(vmem_limit_bytes=1024 * 1024),
    )(*results)


def solution(mesh):
    placed = (P("dp", "rows", None, None), P(), P(), P(), P("dp", "rows", None, None))
    return jax.shard_map(
        body,
        mesh=mesh,
        in_specs=placed,
        out_specs=(P("dp", "rows", None, None), P("dp", "rows", None, None), P(), P()),
        check_vma=False,
    )
```
